32 devices in a mesh: var: 2 (over x), lat: 16 (over z, y, core).
Axes of the slice: x: 2, y: 2, z: 4, core: 2. Of those that a mesh axis runs over, the one named last changes fastest.
Arguments:
- grad_grid: bfloat16 [2, 768, 70, 1536], P('var', 'lat'), may hold values from -6 to 6
- remap: float32 [2, 70, 70], P('var'), may hold values from -0.75 to 0.75
- modes: float32 [2, 70, 70], P('var'), may hold values from -0.75 to 0.75
- balance: float32 [70, 70], replicated, may hold values from -0.75 to 0.75
- legendre: float32 [384, 768, 384], P('lat'), may hold values from -0.21875 to 0.21875
- control: float32 [2, 384, 140, 384], P('var', 'lat'), may hold values from -6 to 6
- step_size: float32 [2], P('var'), may hold values from 0.2 to 0.8
- owner_slots: int32 [384], replicated, may hold values from 0 to 383, each once
Outputs:
- updated: float32 [2, 384, 140, 384], P('var', 'lat')
- increment: bfloat16 [2, 768, 70, 1536], P('var', 'lat')
The draws below stay inside these ranges and needn't reach their ends.
Inputs may be any that keep to these rules, and one draw needn't show every extreme that they name: `owner_slots`: each zonal wavenumber below 384 stands in exactly one owner slot; lat index d holds slots d * 24 to (d + 1) * 24 - 1.
All inputs are finite; a program needn't handle non-finite values.
Results may differ from the reference program's by a relative error of at most 0.001.
Values sent between devices are 32-bit elements; how exact they have to be, the bound alone decides.
No kernel may reach another device: no remote copies, remote signals or barrier semaphores. Data moves between devices by JAX's collectives and lax.ppermute only.
A program may use at most 192 MiB of HBM per device.

```python
import math
import jax
import jax.numpy as jnp
from jax import lax

NLON = 1536
NLAT = 768
LEV = 70
M = 384
NN = 384
N_LAT = 16


def levels(own_key, extent, split, least, top_value):
    level = 1.0
    for axis_at, shards_of in split:
        heights = jax.random.uniform(jax.random.fold_in(jax.random.fold_in(own_key, 6), axis_at), (shards_of,), jnp.float32, least / len(split), top_value / len(split))
        level = level * jnp.repeat(jnp.exp(heights), extent[axis_at] // shards_of).reshape((-1,) + (1,) * (len(extent) - 1 - axis_at))
    return level


def bell_draw(rng, extent, spread, most, split=(), kind=jnp.bfloat16):
    level = levels(rng, extent, split, -0.22, 0.18) if split else 1.0
    entries = jax.random.normal(rng, extent, jnp.float32) * spread * level
    return jnp.minimum(jnp.maximum(entries, -most), most).astype(kind)


def setup_inputs(seed: int = 0) -> dict:
    splits = jax.random.split(jax.random.key(seed), 9)
    return {
        "grad_grid": bell_draw(splits[0], (2, NLAT, LEV, NLON), 1.0, 6.0, ((0, 2), (1, 16))),
        "remap": bell_draw(splits[1], (2, LEV, LEV), LEV ** -0.5, 0.75, ((0, 2),), jnp.float32),
        "modes": bell_draw(splits[2], (2, LEV, LEV), LEV ** -0.5, 0.75, ((0, 2),), jnp.float32),
        "balance": bell_draw(splits[3], (LEV, LEV), LEV ** -0.5, 0.75, (), jnp.float32),
        "legendre": bell_draw(splits[4], (M, NLAT, NN), NLAT ** -0.5, 0.21875, ((0, 16),), jnp.float32),
        "control": bell_draw(splits[5], (2, M, 2 * LEV, NN), 1.0, 6.0, ((0, 2), (1, 16)), jnp.float32),
        "step_size": jnp.clip(0.2 + 0.6 * jax.random.uniform(splits[6], (2,), jnp.float32) ** levels(splits[6], (2,), ((0, 2),), -0.2, 0.2), 0.2, 0.8),
        "owner_slots": jax.random.permutation(splits[7], M).astype(jnp.int32),
    }


highest = lax.Precision.HIGHEST

def make_waves(owner_slots, lon_count):
    longitude = lax.iota(jnp.int32, lon_count)
    phases = longitude[:, None] * owner_slots[None, :].astype(jnp.int32) % lon_count
    angles = phases.astype(jnp.float32) * (2.0 * math.pi / lon_count)
    factor = math.sqrt(2.0 / lon_count)
    return jnp.stack([jnp.cos(angles), jnp.sin(angles)], axis=1) * factor

def reference(grad_grid, remap, modes, balance, legendre, control, step_size, owner_slots):
    wave_table = make_waves(owner_slots, NLON)
    lat_block = NLAT // N_LAT
    spectral_adj = []
    for variable in range(2):

        def grid_block(lat_piece, variable=variable):
            lifted = jnp.einsum('ik,lij->lkj', remap[variable], lat_piece.astype(jnp.float32), precision=highest)
            return jnp.einsum('lkj,jcs->slck', lifted, wave_table, precision=highest)
        pieces = lax.map(grid_block, grad_grid[variable].reshape(N_LAT, lat_block, LEV, NLON))
        fourier_adj = jnp.transpose(pieces, (1, 0, 2, 3, 4)).reshape(M, NLAT, 2 * LEV)
        coef = jnp.einsum('sln,slq->sqn', legendre, fourier_adj, precision=highest)
        spectral_adj.append(coef.reshape(M, 2, LEV, NN))
    carried = spectral_adj[0] + jnp.einsum('ik,scin->sckn', balance, spectral_adj[1], precision=highest)
    mode_psi = jnp.einsum('ik,scin->sckn', modes[0], carried, precision=highest)
    mode_mass = jnp.einsum('ik,scin->sckn', modes[1], spectral_adj[1], precision=highest)
    mode_adj = [mode_psi.reshape(M, 2 * LEV, NN), mode_mass.reshape(M, 2 * LEV, NN)]
    updated = [control[v] - step_size[v] * (control[v] + mode_adj[v]) for v in range(2)]
    coef_psi = jnp.einsum('ki,scin->sckn', modes[0], updated[0].reshape(M, 2, LEV, NN), precision=highest)
    coef_mass = jnp.einsum('ki,scin->sckn', modes[1], updated[1].reshape(M, 2, LEV, NN), precision=highest)
    coef_mass = coef_mass + jnp.einsum('ki,scin->sckn', balance, coef_psi, precision=highest)
    level_coef = [coef_psi, coef_mass]
    increments = []
    for variable in range(2):
        fourier = jnp.einsum('sln,sqn->slq', legendre, level_coef[variable].reshape(M, 2 * LEV, NN), precision=highest)
        blocks = jnp.transpose(fourier.reshape(M, N_LAT, lat_block, 2, LEV), (1, 0, 2, 3, 4))

        def wave_block(coef_piece, variable=variable):
            lowered = jnp.einsum('slck,jcs->lkj', coef_piece, wave_table, precision=highest)
            return jnp.einsum('ik,lkj->lij', remap[variable], lowered, precision=highest).astype(jnp.bfloat16)
        grid_out = lax.map(wave_block, blocks)
        increments.append(grid_out.reshape(NLAT, LEV, NLON))
    return (jnp.stack(updated), jnp.stack(increments))
```

```python
import copy
import functools
import math

import jax
import jax.numpy as jnp
import numpy as np
from jax import lax
from jax.experimental import pallas as pl
from jax.experimental.pallas import tpu as pltpu
from jax.sharding import PartitionSpec as P

highest = lax.Precision.HIGHEST
LANES = 128
COST_SHARE = 8
VMEM_BYTES = 63 * 1024 * 1024
NN = (((1,), (0,)), ((), ()))
NT = (((1,), (1,)), ((), ()))


def round_up(value, step):
    return -(-value // step) * step


def from_behind(block, axis, distance):
    devices = range(lax.axis_size(axis))
    route = [(i - distance, i) for i in devices if i - distance in devices]
    return lax.ppermute(block, axis, route)


@functools.lru_cache(maxsize=None)
def natural_waves(wave_count, lon_count):
    phases = np.arange(wave_count)[:, None] * np.arange(lon_count)[None, :] % lon_count
    angles = phases * (2.0 * math.pi / lon_count)
    table = np.stack([np.cos(angles), np.sin(angles)], axis=1) * math.sqrt(2.0 / lon_count)
    table = table.reshape(2 * wave_count, lon_count).astype(np.float32)
    upper = table.astype(jnp.bfloat16)
    lower = (table - upper.astype(np.float32)).astype(jnp.bfloat16)
    return np.concatenate([upper, lower], axis=1)


def chosen_waves(slots, wave_count, lon_count):
    rows = (2 * slots[:, None] + lax.iota(jnp.int32, 2)[None, :]).reshape(-1)
    onehot = (rows[:, None] == lax.iota(jnp.int32, 2 * wave_count)[None, :]).astype(jnp.bfloat16)
    table = jnp.asarray(natural_waves(wave_count, lon_count))
    return jnp.dot(onehot, table, preferred_element_type=jnp.float32).astype(jnp.bfloat16)


def halves(x):
    upper = x.astype(jnp.bfloat16)
    return upper, (x - upper.astype(jnp.float32)).astype(jnp.bfloat16)


def mxu(a, b, dims):
    return lax.dot_general(a, b, dims, preferred_element_type=jnp.float32)


def dot3(a, b, dims=NN):
    (a_up, a_low), (b_up, b_low) = a, b
    return mxu(a_up, b_up, dims) + (mxu(a_up, b_low, dims) + mxu(a_low, b_up, dims))


def anywhere(arrays):
    return [pl.BlockSpec(memory_space=pl.ANY)] * len(arrays)


def behind(kernel, inputs, after):
    def body(*refs):
        kernel(*refs[:inputs], *refs[inputs + after :])

    return body


MARK = jax.ShapeDtypeStruct((8, LANES), jnp.float32)
MARK_SPEC = pl.BlockSpec(MARK.shape, lambda *_: (0, 0))


def cost(flops):
    return pl.CostEstimate(flops=flops // COST_SHARE, bytes_accessed=0, transcendentals=0)


def gate(block, *after):
    return pl.pallas_call(
        lambda *refs: None,
        in_specs=anywhere((block, *after)),
        out_specs=pl.BlockSpec(memory_space=pl.ANY),
        out_shape=jax.ShapeDtypeStruct(block.shape, block.dtype),
        input_output_aliases={0: 0},
        cost_estimate=pl.CostEstimate(flops=0, bytes_accessed=0, transcendentals=0),
        name="gate",
    )(block, *after)


class Rows:
    def __init__(self, lats, levels, units):
        self.levels, self.units = levels, units
        self.full = lats * levels // LANES * LANES
        self.tail = lats * levels - self.full
        self.lanes = units * self.full + round_up(units * self.tail, LANES)

    def end(self, unit):
        return self.units * self.full + unit * self.tail

    def pieces(self, unit, lat):
        first, last = lat * self.levels, (lat + 1) * self.levels
        pieces = []
        if first < self.full:
            stop = min(last, self.full)
            pieces.append((slice(unit * self.full + first, unit * self.full + stop), slice(0, stop - first)))
        if last > self.full:
            start = max(first, self.full)
            lane = self.end(unit) + start - self.full
            pieces.append((slice(lane, lane + last - start), slice(start - first, self.levels)))
        return pieces


def dft_kernel(steps, place, grad_ref, wave_ref, out_ref, mark_ref, rows_ref):
    mark_ref[...] = jnp.zeros(mark_ref.shape, jnp.float32)
    levels, lats, lons = grad_ref.shape
    waves = wave_ref.shape[0]
    lead = rows_ref.shape[1] // lats
    grad = grad_ref[...].reshape(levels * lats, lons)
    terms = mxu(grad, jnp.concatenate([wave_ref[:, :lons], wave_ref[:, lons:]], axis=0), NT)
    coef = terms[:, :waves] + terms[:, waves:]
    for unit in range(place.units):
        rows_ref[unit, 0 : levels * lats, :] = coef[:, unit * LANES : (unit + 1) * LANES]
        if lead > levels:
            rows_ref[unit, levels * lats :, :] = jnp.zeros(((lead - levels) * lats, LANES), jnp.float32)

    for step in range(steps):

        @pl.when(pl.program_id(0) == step)
        def _(step=step):
            if step == 0:
                end = place.end(place.units)
                out_ref[:, end:] = jnp.zeros((LANES, place.lanes - end), jnp.float32)
            for unit in range(place.units):
                for lat in range(lats):
                    part = rows_ref[unit, pl.ds(lat, lead, stride=lats), :].T
                    for lanes, chosen in place.pieces(unit, step * lats + lat):
                        out_ref[:, lanes] = part[:, chosen]


def forward_dft(grad, table, place, after):
    levels, lats, lons = grad.shape
    waves = table.shape[0]
    block = 16
    steps = lats // block
    lead = round_up(levels, 8)
    return pl.pallas_call(
        behind(functools.partial(dft_kernel, steps, place), 2, len(after)),
        grid=(steps,),
        in_specs=[
            pl.BlockSpec((levels, block, lons), lambda i: (0, i, 0)),
            pl.BlockSpec(table.shape, lambda i: (0, 0)),
            *anywhere(after),
        ],
        out_specs=[pl.BlockSpec((LANES, place.lanes), lambda i: (0, 0)), MARK_SPEC],
        out_shape=[jax.ShapeDtypeStruct((LANES, place.lanes), jnp.float32), MARK],
        scratch_shapes=[pltpu.VMEM((place.units, lead * block, LANES), jnp.float32)],
        compiler_params=pltpu.CompilerParams(vmem_limit_bytes=VMEM_BYTES),
        cost_estimate=cost(4 * levels * lats * lons * waves),
        name="forward_dft",
    )(grad, table, *after)


def spectral_kernel(place, got_ref, end_ref, leg_ref, mat_ref, own_ref, send_ref, flat_ref, cols_ref):
    devices, rows, width = got_ref.shape
    slots, lat_count, _ = leg_ref.shape
    lats = lat_count // devices
    lead = mat_ref.shape[1] // 2
    levels = place.levels
    tiles = width // LANES
    cols_ref[...] = jnp.zeros(cols_ref.shape, jnp.float32)
    for tile in range(tiles):
        piece = got_ref[:, :, tile * LANES : (tile + 1) * LANES]
        flat_ref[tile] = piece.reshape(devices * rows, LANES)
    flat_ref[tiles] = end_ref[...].reshape(devices * rows, LANES)
    mat = halves(mat_ref[...])
    for slot in range(slots):
        turned = []
        for part in range(2):
            row = 2 * slot + part
            lines = [flat_ref[t, pl.ds(row, devices, stride=rows), :] for t in range(tiles + 1)]
            end = place.end(place.unit) % LANES
            lines[tiles] = lines[tiles][:, end : end + place.tail]
            line = jnp.concatenate(lines, axis=1)
            for lat in range(lats):
                cols_ref[pl.ds(row * lat_count + lat, devices, stride=lats), 0:levels] = line[
                    :, lat * levels : (lat + 1) * levels
                ]
            turned.append(cols_ref[row * lat_count : (row + 1) * lat_count, :].T[:lead])
        coef = dot3(halves(jnp.concatenate(turned, axis=0)), halves(leg_ref[slot]))
        mixed = dot3(mat, halves(coef))
        own_ref[slot] = mixed[: 2 * lead]
        send_ref[slot] = mixed[2 * lead :]


def spectral(got, place, unit, legendre, first, mat, after):
    devices, rows, _ = got.shape
    _, lat_count, degrees = legendre.shape
    slots = rows // 2
    lead = mat.shape[1]
    place = copy.copy(place)
    place.unit = unit
    end_tile = place.end(unit) // LANES
    shape = jax.ShapeDtypeStruct((slots, lead, degrees), jnp.float32)
    spec = pl.BlockSpec(shape.shape, lambda i: (0, 0, 0))
    return pl.pallas_call(
        behind(functools.partial(spectral_kernel, place), 4, len(after)),
        grid=(1,),
        in_specs=[
            pl.BlockSpec((devices, rows, place.full), lambda i: (0, 0, unit)),
            pl.BlockSpec((devices, rows, LANES), lambda i: (0, 0, end_tile)),
            pl.BlockSpec((slots, lat_count, degrees), lambda i: (first, 0, 0)),
            pl.BlockSpec(mat.shape, lambda i: (0, 0)),
            *anywhere(after),
        ],
        out_specs=[spec, spec],
        out_shape=[shape, shape],
        scratch_shapes=[
            pltpu.VMEM((place.full // LANES + 1, devices * rows, LANES), jnp.float32),
            pltpu.VMEM((rows * lat_count, LANES), jnp.float32),
        ],
        compiler_params=pltpu.CompilerParams(vmem_limit_bytes=VMEM_BYTES),
        cost_estimate=cost(12 * slots * lat_count * degrees * lead),
        name="spectral_adjoint",
    )(got, got, legendre, mat, *after)


def update_kernel(step_ref, own_ref, got_ref, control_ref, mode_ref, mat_ref, new_ref, keep_ref, send_ref):
    lead = own_ref.shape[1]
    mode = halves(mode_ref[...])
    mat = halves(mat_ref[...])
    for slot in range(own_ref.shape[0]):
        adjoint = dot3(mode, halves(own_ref[slot] + got_ref[slot]))
        control = control_ref[slot]
        new = control - step_ref[0] * (control + adjoint)
        new_ref[slot] = new
        mixed = dot3(mat, halves(new))
        keep_ref[slot] = mixed[:lead]
        send_ref[slot] = mixed[lead:]


def update(step_size, own, got, control, first, mode, mat, after):
    slots, lead, degrees = own.shape
    spec = pl.BlockSpec(own.shape, lambda i: (0, 0, 0))
    shape = jax.ShapeDtypeStruct(own.shape, jnp.float32)
    return pl.pallas_call(
        behind(update_kernel, 6, len(after)),
        grid=(1,),
        in_specs=[
            pl.BlockSpec(memory_space=pltpu.SMEM),
            spec,
            spec,
            pl.BlockSpec(own.shape, lambda i: (first, 0, 0)),
            pl.BlockSpec(mode.shape, lambda i: (0, 0)),
            pl.BlockSpec(mat.shape, lambda i: (0, 0)),
            *anywhere(after),
        ],
        out_specs=[spec, spec, spec],
        out_shape=[shape, shape, shape],
        compiler_params=pltpu.CompilerParams(vmem_limit_bytes=VMEM_BYTES),
        cost_estimate=cost(36 * slots * lead * lead * degrees),
        name="gradient_step",
    )(step_size, own, got, control, mode, mat, *after)


def back_kernel(place, *refs):
    units = place.units
    keep_refs, got_refs = refs[:units], refs[units : 2 * units]
    leg_ref, mat_ref, out_ref, mark_ref, cols_ref, line_ref, flat_ref = refs[2 * units :]
    mark_ref[...] = jnp.zeros(mark_ref.shape, jnp.float32)
    devices, rows, _ = out_ref.shape
    slots, lat_count, degrees = leg_ref.shape
    lats = lat_count // devices
    lead = mat_ref.shape[0] // 2
    levels = place.levels
    tiles = place.full // LANES
    mat = halves(mat_ref[...])
    gap = jnp.zeros((LANES - lead, degrees), jnp.float32)

    for unit in range(units):

        @pl.when(pl.program_id(0) == unit)
        def _(unit=unit):
            if unit == 0:
                out_ref[:, :, units * place.full :] = jnp.zeros(
                    (devices, rows, place.lanes - units * place.full), jnp.float32
                )
            if place.tail:
                unused = (line_ref.shape[0], LANES - place.tail)
                line_ref[:, place.full + place.tail :] = jnp.zeros(unused, jnp.float32)
            for slot in range(slots):
                coef = dot3(mat, halves(keep_refs[unit][slot] + got_refs[unit][slot]))
                coef = jnp.concatenate([coef[:lead], gap, coef[lead:], gap], axis=0)
                fourier = dot3(halves(leg_ref[slot]), halves(coef), NT)
                for part in range(2):
                    row = 2 * slot + part
                    base = row * lat_count
                    cols_ref[base : base + lat_count, :] = fourier[:, part * LANES : (part + 1) * LANES]
                    line = slice(row * devices, (row + 1) * devices)
                    for lat in range(lats):
                        piece = cols_ref[pl.ds(base + lat, devices, stride=lats), :]
                        line_ref[line, lat * levels : (lat + 1) * levels] = piece[:, :levels]
                    for tile in range(line_ref.shape[1] // LANES):
                        flat_ref[tile, pl.ds(row, devices, stride=rows), :] = line_ref[
                            line, tile * LANES : (tile + 1) * LANES
                        ]
            for tile in range(tiles):
                start = unit * place.full + tile * LANES
                out_ref[:, :, start : start + LANES] = flat_ref[tile].reshape(devices, rows, LANES)
            if place.tail:
                lane = place.end(unit)
                ends = flat_ref[tiles].reshape(devices, rows, LANES)[:, :, : place.tail]
                out_ref[:, :, lane : lane + place.tail] = ends


def spectral_back(keeps, gots, place, legendre, first, mat, devices, after):
    slots, lead, degrees = keeps[0].shape
    lat_count = legendre.shape[1]
    rows = 2 * slots
    units = place.units
    spec = pl.BlockSpec(keeps[0].shape, lambda i: (0, 0, 0))
    padded_row = place.full + (LANES if place.tail else 0)
    shape = jax.ShapeDtypeStruct((devices, rows, place.lanes), jnp.float32)
    return pl.pallas_call(
        behind(functools.partial(back_kernel, place), 2 * units + 2, len(after)),
        grid=(units,),
        in_specs=[spec] * (2 * units)
        + [
            pl.BlockSpec((slots, lat_count, degrees), lambda i: (i + first, 0, 0)),
            pl.BlockSpec(mat.shape, lambda i: (0, 0)),
            *anywhere(after),
        ],
        out_specs=[pl.BlockSpec(shape.shape, lambda i: (0, 0, 0)), MARK_SPEC],
        out_shape=[shape, MARK],
        scratch_shapes=[
            pltpu.VMEM((rows * lat_count, LANES), jnp.float32),
            pltpu.VMEM((rows * devices, padded_row), jnp.float32),
            pltpu.VMEM((padded_row // LANES, devices * rows, LANES), jnp.float32),
        ],
        compiler_params=pltpu.CompilerParams(vmem_limit_bytes=VMEM_BYTES),
        cost_estimate=cost(12 * units * slots * lat_count * degrees * lead),
        name="spectral_forward",
    )(*keeps, *gots, legendre, mat, *after)


def inverse_kernel(steps, place, has_total, coef_ref, up_ref, low_ref, *refs):
    total_ref = refs[0] if has_total else None
    out_ref, rows_ref, left_ref = refs[has_total:]
    levels, lats, columns = out_ref.shape
    waves = up_ref.shape[0]

    for step in range(steps):

        @pl.when((pl.program_id(0) == step) & (pl.program_id(1) == 0))
        def _(step=step):
            for unit in range(place.units):
                for lat in range(lats):
                    parts = [coef_ref[:, at] for at, _ in place.pieces(unit, step * lats + lat)]
                    part = parts[0] if len(parts) == 1 else jnp.concatenate(parts, axis=1)
                    rows_ref[unit, pl.ds(lat, levels, stride=lats), :] = part.T
                high, rest = halves(rows_ref[unit])
                for term, value in enumerate((high, rest, high)):
                    start = term * waves + unit * LANES
                    left_ref[:, start : start + LANES] = value

    right = jnp.concatenate([up_ref[...], up_ref[...], low_ref[...]], axis=0)
    result = mxu(left_ref[...], right, NN).reshape(levels, lats, columns)
    if has_total:
        result = result + total_ref[...]
    out_ref[...] = result.astype(out_ref.dtype)


def inverse_dft(coef, place, table, total, lats, dtype, after):
    waves = table.shape[0]
    lons = table.shape[1] // 2
    levels = place.levels
    block = 16
    steps = lats // block
    columns = 512 if lons % 512 == 0 else lons
    turns = lons // columns
    grid_spec = pl.BlockSpec((levels, block, columns), lambda i, j: (0, i, j))
    totals = [] if total is None else [total]
    return pl.pallas_call(
        behind(functools.partial(inverse_kernel, steps, place, len(totals)), 3 + len(totals), len(after)),
        grid=(steps, turns),
        in_specs=[
            pl.BlockSpec(coef.shape, lambda i, j: (0, 0)),
            pl.BlockSpec((waves, columns), lambda i, j: (0, j)),
            pl.BlockSpec((waves, columns), lambda i, j: (0, j + turns)),
        ]
        + [grid_spec] * len(totals)
        + anywhere(after),
        out_specs=grid_spec,
        out_shape=jax.ShapeDtypeStruct((levels, lats, lons), dtype),
        scratch_shapes=[
            pltpu.VMEM((place.units, levels * block, LANES), jnp.float32),
            pltpu.VMEM((levels * block, 3 * waves), jnp.bfloat16),
        ],
        compiler_params=pltpu.CompilerParams(vmem_limit_bytes=VMEM_BYTES),
        cost_estimate=cost(6 * levels * lats * lons * waves),
        name="inverse_dft",
    )(coef, table, table, *totals, *after)


def padded(matrix, lead):
    return jnp.pad(matrix, ((0, lead - matrix.shape[0]), (0, lead - matrix.shape[1])))


def on_both(matrix, lead):
    return jnp.kron(jnp.eye(2, dtype=jnp.float32), padded(matrix, lead))


def exchange(block):
    return lax.all_to_all(block, "lat", split_axis=0, concat_axis=0, tiled=True)


def tiled_local(grad_grid, remap, modes, balance, legendre, control, step_size, owner_slots):
    _, lats, levels, lons = grad_grid.shape
    owned, _, degrees = legendre.shape
    wave_count = owner_slots.shape[0]
    devices = wave_count // owned
    lead = round_up(levels, 8)
    grad = jnp.transpose(grad_grid[0], (1, 0, 2))
    units = owned // 4
    sizes = [2, units - 3, 1] if units > 3 else [units]
    place = [Rows(lats, levels, size) for size in sizes]
    members, first = [], 0
    for size in sizes:
        members.append(list(range(first, first + size)))
        first += size
    by_owner = owner_slots.reshape(devices, units, 4).transpose(1, 0, 2)

    waves = [chosen_waves(by_owner[m[0] : m[-1] + 1].reshape(-1), wave_count, lons) for m in members]
    mix = functools.partial(jnp.einsum, precision=highest)
    adjoint_mat = jnp.concatenate(
        [on_both(remap[0].T, lead), on_both(mix("ik,kj->ji", remap[0], balance), lead)]
    )
    mode_mat = on_both(modes[0].T, lead)
    forward_mat = jnp.concatenate(
        [on_both(modes[0], lead), on_both(mix("ik,kj->ij", balance, modes[0]), lead)]
    )
    remap_mat = on_both(remap[0], lead)
    own_control = control[0].reshape(owned, 2, levels, degrees)
    own_control = jnp.pad(own_control, ((0, 0), (0, 0), (0, lead - levels), (0, 0)))
    own_control = own_control.reshape(owned, 2 * lead, degrees)
    own, send, other, new, keep, back_send, back_other = ({} for _ in range(7))

    def dft(c, *after):
        coef, mark = forward_dft(grad, waves[c], place[c], after)
        return coef.reshape(devices, 8, place[c].lanes), mark

    def adjoint(c, got, *after):
        for at, u in enumerate(members[c]):
            own[u], send[u] = spectral(got, place[c], at, legendre, u, adjoint_mat, after)
            other[u] = from_behind(send[u], "var", -1)

    def gradient_step(c, *after):
        for u in members[c]:
            new[u], keep[u], back_send[u] = update(
                step_size, own[u], other[u], own_control, u, mode_mat, forward_mat, after
            )
            back_other[u] = from_behind(back_send[u], "var", 1)

    def forward(c, *after):
        keeps, gots = [keep[u] for u in members[c]], [back_other[u] for u in members[c]]
        return spectral_back(
            keeps, gots, place[c], legendre, members[c][0], remap_mat, devices, after
        )

    def inverse(c, arrived, total, dtype, *after):
        coef = arrived.reshape(LANES, place[c].lanes)
        return inverse_dft(coef, place[c], waves[c], total, lats, dtype, after)

    def all_new():
        updated = jnp.concatenate([new[u] for u in range(units)]).reshape(owned, 2, lead, degrees)
        return updated[:, :, :levels].reshape(owned, 2 * levels, degrees)

    if len(sizes) == 3:
        coef_a, _ = dft(0)
        got_a = exchange(coef_a)
        coef_b, _ = dft(1)
        coef_c, mark = dft(2)
        got_b = exchange(gate(coef_b, got_a, mark))
        adjoint(0, got_a)
        gradient_step(0)
        back_a, mark = forward(0)
        got_c = exchange(gate(coef_c, got_b, mark))
        adjoint(1, got_b)
        arrived_a = exchange(gate(back_a, got_c, *[own[u] for u in members[1]], other[members[1][0]]))
        adjoint(2, got_c)
        gradient_step(1)
        back_b, _ = forward(1, own[members[2][0]])
        arrived_b = exchange(gate(back_b, arrived_a, own[members[2][0]]))
        gradient_step(2, arrived_a)
        updated = all_new()
        back_c, _ = forward(2)
        total = inverse(0, arrived_a, None, jnp.float32)
        arrived_c = exchange(gate(back_c, arrived_b, total, updated))
        total = inverse(1, arrived_b, total, jnp.float32)
        total = inverse(2, arrived_c, total, jnp.bfloat16)
    else:
        coef, _ = dft(0)
        adjoint(0, exchange(coef))
        gradient_step(0)
        updated = all_new()
        back, _ = forward(0)
        total = inverse(0, exchange(back), None, jnp.bfloat16)
    increment = jnp.transpose(total, (1, 0, 2))
    return (updated[None], increment[None])


def make_waves(owner_slots, lon_count):
    longitude = lax.iota(jnp.int32, lon_count)
    phases = longitude[:, None] * owner_slots[None, :] % lon_count
    angles = phases.astype(jnp.float32) * (2.0 * math.pi / lon_count)
    factor = math.sqrt(2.0 / lon_count)
    return jnp.stack([jnp.cos(angles), jnp.sin(angles)], axis=1) * factor


def plain_local(grad_grid, remap, modes, balance, legendre, control, step_size, owner_slots):
    lat_rows = grad_grid.shape[1]
    levels = grad_grid.shape[2]
    lon_count = grad_grid.shape[3]
    wave_count = owner_slots.shape[0]
    owned_count = legendre.shape[0]
    degrees = legendre.shape[2]
    wave_table = make_waves(owner_slots, lon_count)
    remap_var = remap[0]
    modes_var = modes[0]
    lifted = jnp.einsum(
        "ik,lij->lkj", remap_var, grad_grid[0].astype(jnp.float32), precision=highest
    )
    slab_coef = jnp.einsum("lkj,jcs->slck", lifted, wave_table, precision=highest)
    spectral_coef = jnp.einsum(
        "sln,slq->sqn",
        legendre,
        lax.all_to_all(
            slab_coef.reshape(wave_count, lat_rows, 2 * levels),
            "lat",
            split_axis=0,
            concat_axis=1,
            tiled=True,
        ),
        precision=highest,
    )
    spec_four = spectral_coef.reshape(owned_count, 2, levels, degrees)
    partner = from_behind(spec_four, "var", -1)
    blended = spec_four + jnp.einsum("ik,scin->sckn", balance, partner, precision=highest)
    spectral_coef = jnp.einsum("ik,scin->sckn", modes_var, blended, precision=highest).reshape(
        owned_count, 2 * levels, degrees
    )
    own_control = control[0]
    updated = own_control - step_size[0] * (own_control + spectral_coef)
    level_coef = jnp.einsum(
        "ki,scin->sckn",
        modes_var,
        updated.reshape(owned_count, 2, levels, degrees),
        precision=highest,
    )
    partner = from_behind(level_coef, "var", 1)
    level_coef = level_coef + jnp.einsum("ki,scin->sckn", balance, partner, precision=highest)
    level_coef = level_coef.reshape(owned_count, 2 * levels, degrees)
    fourier = jnp.einsum("sln,sqn->slq", legendre, level_coef, precision=highest)
    slab_back = lax.all_to_all(fourier, "lat", split_axis=1, concat_axis=0, tiled=True)
    slab_back = slab_back.reshape(wave_count, lat_rows, 2, levels)
    lowered = jnp.einsum("slck,jcs->lkj", slab_back, wave_table, precision=highest)
    increment = jnp.einsum("ik,lkj->lij", remap_var, lowered, precision=highest).astype(
        jnp.bfloat16
    )
    return (updated[None], increment[None])


def local(*arrays):
    grad_grid, legendre = arrays[0], arrays[4]
    devices = legendre.shape[1] // grad_grid.shape[1]
    levels = grad_grid.shape[2]
    tail = grad_grid.shape[1] * levels % LANES
    fits = (
        legendre.shape[0] % 4 == 0
        and grad_grid.shape[1] % 16 == 0
        and devices * 8 == LANES
        and round_up(levels, 8) <= LANES
        and tail > 0
        and LANES % tail == 0
    )
    return (tiled_local if fits else plain_local)(*arrays)


def solution(mesh):
    return jax.shard_map(
        local,
        mesh=mesh,
        in_specs=(
            P("var", "lat", None, None),
            P("var", None, None),
            P("var", None, None),
            P(),
            P("lat", None, None),
            P("var", "lat", None, None),
            P("var"),
            P(),
        ),
        out_specs=(P("var", "lat", None, None), P("var", "lat", None, None)),
        check_vma=False,
    )
```

```python
import copy
import functools
import math

import jax
import jax.numpy as jnp
from jax import lax
from jax.experimental import pallas as pl
from jax.experimental.pallas import tpu as pltpu
from jax.sharding import PartitionSpec as P

highest = lax.Precision.HIGHEST
LANES = 128
COST_SHARE = 8
VMEM_BYTES = 63 * 1024 * 1024
NN = (((1,), (0,)), ((), ()))
NT = (((1,), (1,)), ((), ()))


def round_up(value, step):
    return -(-value // step) * step


def from_behind(block, axis, distance):
    devices = range(lax.axis_size(axis))
    route = [(i - distance, i) for i in devices if i - distance in devices]
    return lax.ppermute(block, axis, route)


def sine(x):
    square = x * x
    tail = 1.0
    for divisor in (156, 110, 72, 42, 20, 6):
        tail = 1.0 - square * (tail * (1.0 / divisor))
    return x * tail


def wave_rows(slots, lons):
    shape = (slots.shape[0], lons)
    lon = lax.broadcasted_iota(jnp.int32, shape, 1)
    part = lax.broadcasted_iota(jnp.int32, shape, 0) % 2
    phase = (slots * lon - part * (lons // 4)).astype(jnp.float32)
    phase = phase - jnp.floor(phase * (1.0 / lons)) * lons
    half = sine((phase - lons / 2) * (math.pi / lons))
    return (2.0 * half * half - 1.0) * math.sqrt(2.0 / lons)


def halves(x):
    upper = x.astype(jnp.bfloat16)
    return upper, (x - upper.astype(jnp.float32)).astype(jnp.bfloat16)


def mxu(a, b, dims):
    return lax.dot_general(a, b, dims, preferred_element_type=jnp.float32)


def dot3(a, b, dims=NN):
    (a_up, a_low), (b_up, b_low) = a, b
    return mxu(a_up, b_up, dims) + (mxu(a_up, b_low, dims) + mxu(a_low, b_up, dims))


def anywhere(arrays):
    return [pl.BlockSpec(memory_space=pl.ANY)] * len(arrays)


def behind(kernel, inputs, after):
    def body(*refs):
        kernel(*refs[:inputs], *refs[inputs + after :])

    return body


MARK = jax.ShapeDtypeStruct((8, LANES), jnp.float32)
MARK_SPEC = pl.BlockSpec(MARK.shape, lambda *_: (0, 0))


def cost(flops):
    return pl.CostEstimate(flops=flops // COST_SHARE, bytes_accessed=0, transcendentals=0)


def gate(block, *after):
    return pl.pallas_call(
        lambda *refs: None,
        in_specs=anywhere((block, *after)),
        out_specs=pl.BlockSpec(memory_space=pl.ANY),
        out_shape=jax.ShapeDtypeStruct(block.shape, block.dtype),
        input_output_aliases={0: 0},
        cost_estimate=pl.CostEstimate(flops=0, bytes_accessed=0, transcendentals=0),
        name="gate",
    )(block, *after)


class Rows:
    def __init__(self, lats, levels, units):
        self.levels, self.units = levels, units
        self.full = lats * levels // LANES * LANES
        self.tail = lats * levels - self.full
        self.lanes = units * self.full + round_up(units * self.tail, LANES)

    def end(self, unit):
        return self.units * self.full + unit * self.tail

    def pieces(self, unit, lat):
        first, last = lat * self.levels, (lat + 1) * self.levels
        pieces = []
        if first < self.full:
            stop = min(last, self.full)
            pieces.append((slice(unit * self.full + first, unit * self.full + stop), slice(0, stop - first)))
        if last > self.full:
            start = max(first, self.full)
            lane = self.end(unit) + start - self.full
            pieces.append((slice(lane, lane + last - start), slice(start - first, self.levels)))
        return pieces


def dft_kernel(steps, place, slot_ref, grad_ref, out_ref, wave_ref, mark_ref, rows_ref):
    mark_ref[...] = jnp.zeros(mark_ref.shape, jnp.float32)
    levels, lats, lons = grad_ref.shape
    waves = wave_ref.shape[0]
    lead = rows_ref.shape[1] // lats

    @pl.when(pl.program_id(0) == 0)
    def _():
        for unit in range(place.units):
            at = slice(unit * LANES, (unit + 1) * LANES)
            wave_ref[at, :lons], wave_ref[at, lons:] = halves(wave_rows(slot_ref[at, :], lons))

    grad = grad_ref[...].reshape(levels * lats, lons)
    terms = mxu(grad, jnp.concatenate([wave_ref[:, :lons], wave_ref[:, lons:]], axis=0), NT)
    coef = terms[:, :waves] + terms[:, waves:]
    for unit in range(place.units):
        rows_ref[unit, 0 : levels * lats, :] = coef[:, unit * LANES : (unit + 1) * LANES]
        if lead > levels:
            rows_ref[unit, levels * lats :, :] = jnp.zeros(((lead - levels) * lats, LANES), jnp.float32)

    for step in range(steps):

        @pl.when(pl.program_id(0) == step)
        def _(step=step):
            if step == 0:
                end = place.end(place.units)
                out_ref[:, end:] = jnp.zeros((LANES, place.lanes - end), jnp.float32)
            for unit in range(place.units):
                for lat in range(lats):
                    part = rows_ref[unit, pl.ds(lat, lead, stride=lats), :].T
                    for lanes, chosen in place.pieces(unit, step * lats + lat):
                        out_ref[:, lanes] = part[:, chosen]


def forward_dft(slots, grad, place, after):
    levels, lats, lons = grad.shape
    waves = slots.shape[0]
    block = 16
    steps = lats // block
    lead = round_up(levels, 8)
    return pl.pallas_call(
        behind(functools.partial(dft_kernel, steps, place), 2, len(after)),
        grid=(steps,),
        in_specs=[
            pl.BlockSpec(slots.shape, lambda i: (0, 0)),
            pl.BlockSpec((levels, block, lons), lambda i: (0, i, 0)),
            *anywhere(after),
        ],
        out_specs=[
            pl.BlockSpec((LANES, place.lanes), lambda i: (0, 0)),
            pl.BlockSpec((waves, 2 * lons), lambda i: (0, 0)),
            MARK_SPEC,
        ],
        out_shape=[
            jax.ShapeDtypeStruct((LANES, place.lanes), jnp.float32),
            jax.ShapeDtypeStruct((waves, 2 * lons), jnp.bfloat16),
            MARK,
        ],
        scratch_shapes=[pltpu.VMEM((place.units, lead * block, LANES), jnp.float32)],
        compiler_params=pltpu.CompilerParams(vmem_limit_bytes=VMEM_BYTES),
        cost_estimate=cost(4 * levels * lats * lons * waves),
        name="forward_dft",
    )(slots, grad, *after)


def spectral_kernel(place, got_ref, end_ref, leg_ref, mat_ref, own_ref, send_ref, flat_ref, cols_ref):
    devices, rows, width = got_ref.shape
    slots, lat_count, _ = leg_ref.shape
    lats = lat_count // devices
    lead = mat_ref.shape[1] // 2
    levels = place.levels
    tiles = width // LANES
    cols_ref[...] = jnp.zeros(cols_ref.shape, jnp.float32)
    for tile in range(tiles):
        piece = got_ref[:, :, tile * LANES : (tile + 1) * LANES]
        flat_ref[tile] = piece.reshape(devices * rows, LANES)
    flat_ref[tiles] = end_ref[...].reshape(devices * rows, LANES)
    mat = halves(mat_ref[...])
    for slot in range(slots):
        turned = []
        for part in range(2):
            row = 2 * slot + part
            lines = [flat_ref[t, pl.ds(row, devices, stride=rows), :] for t in range(tiles + 1)]
            end = place.end(place.unit) % LANES
            lines[tiles] = lines[tiles][:, end : end + place.tail]
            line = jnp.concatenate(lines, axis=1)
            for lat in range(lats):
                cols_ref[pl.ds(row * lat_count + lat, devices, stride=lats), 0:levels] = line[
                    :, lat * levels : (lat + 1) * levels
                ]
            turned.append(cols_ref[row * lat_count : (row + 1) * lat_count, :].T[:lead])
        coef = dot3(halves(jnp.concatenate(turned, axis=0)), halves(leg_ref[slot]))
        mixed = dot3(mat, halves(coef))
        own_ref[slot] = mixed[: 2 * lead]
        send_ref[slot] = mixed[2 * lead :]


def spectral(got, place, unit, legendre, first, mat, after):
    devices, rows, _ = got.shape
    _, lat_count, degrees = legendre.shape
    slots = rows // 2
    lead = mat.shape[1]
    place = copy.copy(place)
    place.unit = unit
    end_tile = place.end(unit) // LANES
    shape = jax.ShapeDtypeStruct((slots, lead, degrees), jnp.float32)
    spec = pl.BlockSpec(shape.shape, lambda i: (0, 0, 0))
    return pl.pallas_call(
        behind(functools.partial(spectral_kernel, place), 4, len(after)),
        grid=(1,),
        in_specs=[
            pl.BlockSpec((devices, rows, place.full), lambda i: (0, 0, unit)),
            pl.BlockSpec((devices, rows, LANES), lambda i: (0, 0, end_tile)),
            pl.BlockSpec((slots, lat_count, degrees), lambda i: (first, 0, 0)),
            pl.BlockSpec(mat.shape, lambda i: (0, 0)),
            *anywhere(after),
        ],
        out_specs=[spec, spec],
        out_shape=[shape, shape],
        scratch_shapes=[
            pltpu.VMEM((place.full // LANES + 1, devices * rows, LANES), jnp.float32),
            pltpu.VMEM((rows * lat_count, LANES), jnp.float32),
        ],
        compiler_params=pltpu.CompilerParams(vmem_limit_bytes=VMEM_BYTES),
        cost_estimate=cost(12 * slots * lat_count * degrees * lead),
        name="spectral_adjoint",
    )(got, got, legendre, mat, *after)


def update_kernel(step_ref, own_ref, got_ref, control_ref, mode_ref, mat_ref, new_ref, keep_ref, send_ref):
    lead = own_ref.shape[1]
    mode = halves(mode_ref[...])
    mat = halves(mat_ref[...])
    for slot in range(own_ref.shape[0]):
        adjoint = dot3(mode, halves(own_ref[slot] + got_ref[slot]))
        control = control_ref[slot]
        new = control - step_ref[0] * (control + adjoint)
        new_ref[slot] = new
        mixed = dot3(mat, halves(new))
        keep_ref[slot] = mixed[:lead]
        send_ref[slot] = mixed[lead:]


def update(step_size, own, got, control, first, mode, mat, after):
    slots, lead, degrees = own.shape
    spec = pl.BlockSpec(own.shape, lambda i: (0, 0, 0))
    shape = jax.ShapeDtypeStruct(own.shape, jnp.float32)
    return pl.pallas_call(
        behind(update_kernel, 6, len(after)),
        grid=(1,),
        in_specs=[
            pl.BlockSpec(memory_space=pltpu.SMEM),
            spec,
            spec,
            pl.BlockSpec(own.shape, lambda i: (first, 0, 0)),
            pl.BlockSpec(mode.shape, lambda i: (0, 0)),
            pl.BlockSpec(mat.shape, lambda i: (0, 0)),
            *anywhere(after),
        ],
        out_specs=[spec, spec, spec],
        out_shape=[shape, shape, shape],
        compiler_params=pltpu.CompilerParams(vmem_limit_bytes=VMEM_BYTES),
        cost_estimate=cost(36 * slots * lead * lead * degrees),
        name="gradient_step",
    )(step_size, own, got, control, mode, mat, *after)


def back_kernel(place, *refs):
    units = place.units
    keep_refs, got_refs = refs[:units], refs[units : 2 * units]
    leg_ref, mat_ref, out_ref, mark_ref, cols_ref, line_ref, flat_ref = refs[2 * units :]
    mark_ref[...] = jnp.zeros(mark_ref.shape, jnp.float32)
    devices, rows, _ = out_ref.shape
    slots, lat_count, degrees = leg_ref.shape
    lats = lat_count // devices
    lead = mat_ref.shape[0] // 2
    levels = place.levels
    tiles = place.full // LANES
    mat = halves(mat_ref[...])
    gap = jnp.zeros((LANES - lead, degrees), jnp.float32)

    for unit in range(units):

        @pl.when(pl.program_id(0) == unit)
        def _(unit=unit):
            if unit == 0:
                out_ref[:, :, units * place.full :] = jnp.zeros(
                    (devices, rows, place.lanes - units * place.full), jnp.float32
                )
            if place.tail:
                unused = (line_ref.shape[0], LANES - place.tail)
                line_ref[:, place.full + place.tail :] = jnp.zeros(unused, jnp.float32)
            for slot in range(slots):
                coef = dot3(mat, halves(keep_refs[unit][slot] + got_refs[unit][slot]))
                coef = jnp.concatenate([coef[:lead], gap, coef[lead:], gap], axis=0)
                fourier = dot3(halves(leg_ref[slot]), halves(coef), NT)
                for part in range(2):
                    row = 2 * slot + part
                    base = row * lat_count
                    cols_ref[base : base + lat_count, :] = fourier[:, part * LANES : (part + 1) * LANES]
                    line = slice(row * devices, (row + 1) * devices)
                    for lat in range(lats):
                        piece = cols_ref[pl.ds(base + lat, devices, stride=lats), :]
                        line_ref[line, lat * levels : (lat + 1) * levels] = piece[:, :levels]
                    for tile in range(line_ref.shape[1] // LANES):
                        flat_ref[tile, pl.ds(row, devices, stride=rows), :] = line_ref[
                            line, tile * LANES : (tile + 1) * LANES
                        ]
            for tile in range(tiles):
                start = unit * place.full + tile * LANES
                out_ref[:, :, start : start + LANES] = flat_ref[tile].reshape(devices, rows, LANES)
            if place.tail:
                lane = place.end(unit)
                ends = flat_ref[tiles].reshape(devices, rows, LANES)[:, :, : place.tail]
                out_ref[:, :, lane : lane + place.tail] = ends


def spectral_back(keeps, gots, place, legendre, first, mat, devices, after):
    slots, lead, degrees = keeps[0].shape
    lat_count = legendre.shape[1]
    rows = 2 * slots
    units = place.units
    spec = pl.BlockSpec(keeps[0].shape, lambda i: (0, 0, 0))
    padded_row = place.full + (LANES if place.tail else 0)
    shape = jax.ShapeDtypeStruct((devices, rows, place.lanes), jnp.float32)
    return pl.pallas_call(
        behind(functools.partial(back_kernel, place), 2 * units + 2, len(after)),
        grid=(units,),
        in_specs=[spec] * (2 * units)
        + [
            pl.BlockSpec((slots, lat_count, degrees), lambda i: (i + first, 0, 0)),
            pl.BlockSpec(mat.shape, lambda i: (0, 0)),
            *anywhere(after),
        ],
        out_specs=[pl.BlockSpec(shape.shape, lambda i: (0, 0, 0)), MARK_SPEC],
        out_shape=[shape, MARK],
        scratch_shapes=[
            pltpu.VMEM((rows * lat_count, LANES), jnp.float32),
            pltpu.VMEM((rows * devices, padded_row), jnp.float32),
            pltpu.VMEM((padded_row // LANES, devices * rows, LANES), jnp.float32),
        ],
        compiler_params=pltpu.CompilerParams(vmem_limit_bytes=VMEM_BYTES),
        cost_estimate=cost(12 * units * slots * lat_count * degrees * lead),
        name="spectral_forward",
    )(*keeps, *gots, legendre, mat, *after)


def inverse_kernel(steps, place, has_total, coef_ref, up_ref, low_ref, *refs):
    total_ref = refs[0] if has_total else None
    out_ref, rows_ref, left_ref = refs[has_total:]
    levels, lats, columns = out_ref.shape
    waves = up_ref.shape[0]

    for step in range(steps):

        @pl.when(pl.program_id(0) == step)
        def _(step=step):
            for unit in range(place.units):
                for lat in range(lats):
                    parts = [coef_ref[:, at] for at, _ in place.pieces(unit, step * lats + lat)]
                    part = parts[0] if len(parts) == 1 else jnp.concatenate(parts, axis=1)
                    rows_ref[unit, pl.ds(lat, levels, stride=lats), :] = part.T
                high, rest = halves(rows_ref[unit])
                for term, value in enumerate((high, rest, high)):
                    start = term * waves + unit * LANES
                    left_ref[:, start : start + LANES] = value

    width = 512 if columns % 512 == 0 else columns
    for first in range(0, columns, width):
        at = slice(first, first + width)
        right = jnp.concatenate([up_ref[:, at], up_ref[:, at], low_ref[:, at]], axis=0)
        result = mxu(left_ref[...], right, NN).reshape(levels, lats, width)
        if has_total:
            result = result + total_ref[:, :, at]
        out_ref[:, :, at] = result.astype(out_ref.dtype)


def inverse_dft(coef, place, table, total, lats, dtype, after):
    waves = table.shape[0]
    lons = table.shape[1] // 2
    levels = place.levels
    block = 16
    steps = lats // block
    grid_spec = pl.BlockSpec((levels, block, lons), lambda i: (0, i, 0))
    totals = [] if total is None else [total]
    return pl.pallas_call(
        behind(functools.partial(inverse_kernel, steps, place, len(totals)), 3 + len(totals), len(after)),
        grid=(steps,),
        in_specs=[
            pl.BlockSpec(coef.shape, lambda i: (0, 0)),
            pl.BlockSpec((waves, lons), lambda i: (0, 0)),
            pl.BlockSpec((waves, lons), lambda i: (0, 1)),
        ]
        + [grid_spec] * len(totals)
        + anywhere(after),
        out_specs=grid_spec,
        out_shape=jax.ShapeDtypeStruct((levels, lats, lons), dtype),
        scratch_shapes=[
            pltpu.VMEM((place.units, levels * block, LANES), jnp.float32),
            pltpu.VMEM((levels * block, 3 * waves), jnp.bfloat16),
        ],
        compiler_params=pltpu.CompilerParams(vmem_limit_bytes=VMEM_BYTES),
        cost_estimate=cost(6 * levels * lats * lons * waves),
        name="inverse_dft",
    )(coef, table, table, *totals, *after)


def padded(matrix, lead):
    return jnp.pad(matrix, ((0, lead - matrix.shape[0]), (0, lead - matrix.shape[1])))


def on_both(matrix, lead):
    return jnp.kron(jnp.eye(2, dtype=jnp.float32), padded(matrix, lead))


def exchange(block):
    return lax.all_to_all(block, "lat", split_axis=0, concat_axis=0, tiled=True)


def tiled_local(grad_grid, remap, modes, balance, legendre, control, step_size, owner_slots):
    _, lats, levels, lons = grad_grid.shape
    owned, _, degrees = legendre.shape
    wave_count = owner_slots.shape[0]
    devices = wave_count // owned
    lead = round_up(levels, 8)
    grad = jnp.transpose(grad_grid[0], (1, 0, 2))
    units = owned // 4
    sizes = [1, units - 3, 2] if units > 3 else [units]
    place = [Rows(lats, levels, size) for size in sizes]
    members, first = [], 0
    for size in sizes:
        members.append(list(range(first, first + size)))
        first += size
    by_owner = owner_slots.reshape(devices, units, 4).transpose(1, 0, 2)

    row_slots = jnp.repeat(by_owner.reshape(units * LANES // 2), 2)[:, None]
    waves = {}
    mix = functools.partial(jnp.einsum, precision=highest)
    adjoint_mat = jnp.concatenate(
        [on_both(remap[0].T, lead), on_both(mix("ik,kj->ji", remap[0], balance), lead)]
    )
    mode_mat = on_both(modes[0].T, lead)
    forward_mat = jnp.concatenate(
        [on_both(modes[0], lead), on_both(mix("ik,kj->ij", balance, modes[0]), lead)]
    )
    remap_mat = on_both(remap[0], lead)
    own_control = control[0].reshape(owned, 2, levels, degrees)
    own_control = jnp.pad(own_control, ((0, 0), (0, 0), (0, lead - levels), (0, 0)))
    own_control = own_control.reshape(owned, 2 * lead, degrees)
    own, send, other, new, keep, back_send, back_other = ({} for _ in range(7))

    def dft(c, *after):
        rows = slice(members[c][0] * LANES, (members[c][-1] + 1) * LANES)
        coef, waves[c], mark = forward_dft(row_slots[rows], grad, place[c], after)
        return coef.reshape(devices, 8, place[c].lanes), mark

    def adjoint(c, got, *after):
        for at, u in enumerate(members[c]):
            own[u], send[u] = spectral(got, place[c], at, legendre, u, adjoint_mat, after)
            other[u] = from_behind(send[u], "var", -1)
            after = (own[u],)

    def gradient_step(c, *after):
        for u in members[c]:
            new[u], keep[u], back_send[u] = update(
                step_size, own[u], other[u], own_control, u, mode_mat, forward_mat, after
            )
            after = (new[u], *[back_other[v] for v in (u - 1,) if v in members[c]])
            back_other[u] = from_behind(back_send[u], "var", 1)

    def forward(c, *after):
        keeps, gots = [keep[u] for u in members[c]], [back_other[u] for u in members[c]]
        return spectral_back(
            keeps, gots, place[c], legendre, members[c][0], remap_mat, devices, after
        )

    def inverse(c, arrived, total, dtype, *after):
        coef = arrived.reshape(LANES, place[c].lanes)
        return inverse_dft(coef, place[c], waves[c], total, lats, dtype, after)

    def all_new():
        updated = jnp.concatenate([new[u] for u in range(units)]).reshape(owned, 2, lead, degrees)
        return updated[:, :, :levels].reshape(owned, 2 * levels, degrees)

    if len(sizes) == 3:
        coef_a, _ = dft(0)
        got_a = exchange(coef_a)
        coef_b, _ = dft(1)
        coef_c, mark = dft(2)
        got_b = exchange(gate(coef_b, got_a, mark))
        adjoint(0, got_a)
        gradient_step(0)
        back_a, mark = forward(0)
        got_c = exchange(gate(coef_c, got_b, mark))
        adjoint(1, got_b)
        gradient_step(1)
        arrived_a = exchange(gate(back_a, got_c, new[members[1][-1]], back_other[members[1][-2]]))
        adjoint(2, got_c)
        back_b, _ = forward(1, own[members[2][-1]])
        arrived_b = exchange(gate(back_b, arrived_a))
        gradient_step(2, arrived_a)
        back_c, _ = forward(2)
        total = inverse(0, arrived_a, None, jnp.float32)
        arrived_c = exchange(gate(back_c, arrived_b, total))
        updated = all_new()
        total = inverse(1, arrived_b, total, jnp.float32)
        total = inverse(2, arrived_c, total, jnp.bfloat16)
    else:
        coef, _ = dft(0)
        adjoint(0, exchange(coef))
        gradient_step(0)
        updated = all_new()
        back, _ = forward(0)
        total = inverse(0, exchange(back), None, jnp.bfloat16)
    increment = jnp.transpose(total, (1, 0, 2))
    return (updated[None], increment[None])


def make_waves(owner_slots, lon_count):
    longitude = lax.iota(jnp.int32, lon_count)
    phases = longitude[:, None] * owner_slots[None, :] % lon_count
    angles = phases.astype(jnp.float32) * (2.0 * math.pi / lon_count)
    factor = math.sqrt(2.0 / lon_count)
    return jnp.stack([jnp.cos(angles), jnp.sin(angles)], axis=1) * factor


def plain_local(grad_grid, remap, modes, balance, legendre, control, step_size, owner_slots):
    lat_rows = grad_grid.shape[1]
    levels = grad_grid.shape[2]
    lon_count = grad_grid.shape[3]
    wave_count = owner_slots.shape[0]
    owned_count = legendre.shape[0]
    degrees = legendre.shape[2]
    wave_table = make_waves(owner_slots, lon_count)
    remap_var = remap[0]
    modes_var = modes[0]
    lifted = jnp.einsum(
        "ik,lij->lkj", remap_var, grad_grid[0].astype(jnp.float32), precision=highest
    )
    slab_coef = jnp.einsum("lkj,jcs->slck", lifted, wave_table, precision=highest)
    spectral_coef = jnp.einsum(
        "sln,slq->sqn",
        legendre,
        lax.all_to_all(
            slab_coef.reshape(wave_count, lat_rows, 2 * levels),
            "lat",
            split_axis=0,
            concat_axis=1,
            tiled=True,
        ),
        precision=highest,
    )
    spec_four = spectral_coef.reshape(owned_count, 2, levels, degrees)
    partner = from_behind(spec_four, "var", -1)
    blended = spec_four + jnp.einsum("ik,scin->sckn", balance, partner, precision=highest)
    spectral_coef = jnp.einsum("ik,scin->sckn", modes_var, blended, precision=highest).reshape(
        owned_count, 2 * levels, degrees
    )
    own_control = control[0]
    updated = own_control - step_size[0] * (own_control + spectral_coef)
    level_coef = jnp.einsum(
        "ki,scin->sckn",
        modes_var,
        updated.reshape(owned_count, 2, levels, degrees),
        precision=highest,
    )
    partner = from_behind(level_coef, "var", 1)
    level_coef = level_coef + jnp.einsum("ki,scin->sckn", balance, partner, precision=highest)
    level_coef = level_coef.reshape(owned_count, 2 * levels, degrees)
    fourier = jnp.einsum("sln,sqn->slq", legendre, level_coef, precision=highest)
    slab_back = lax.all_to_all(fourier, "lat", split_axis=1, concat_axis=0, tiled=True)
    slab_back = slab_back.reshape(wave_count, lat_rows, 2, levels)
    lowered = jnp.einsum("slck,jcs->lkj", slab_back, wave_table, precision=highest)
    increment = jnp.einsum("ik,lkj->lij", remap_var, lowered, precision=highest).astype(
        jnp.bfloat16
    )
    return (updated[None], increment[None])


def local(*arrays):
    grad_grid, legendre = arrays[0], arrays[4]
    devices = legendre.shape[1] // grad_grid.shape[1]
    levels = grad_grid.shape[2]
    tail = grad_grid.shape[1] * levels % LANES
    fits = (
        legendre.shape[0] % 4 == 0
        and grad_grid.shape[1] % 16 == 0
        and devices * 8 == LANES
        and round_up(levels, 8) <= LANES
        and tail > 0
        and grad_grid.shape[3] % 4 == 0
        and LANES % tail == 0
    )
    return (tiled_local if fits else plain_local)(*arrays)


def solution(mesh):
    return jax.shard_map(
        local,
        mesh=mesh,
        in_specs=(
            P("var", "lat", None, None),
            P("var", None, None),
            P("var", None, None),
            P(),
            P("lat", None, None),
            P("var", "lat", None, None),
            P("var"),
            P(),
        ),
        out_specs=(P("var", "lat", None, None), P("var", "lat", None, None)),
        check_vma=False,
    )
```

```python
import copy
import functools
import math

import jax
import jax.numpy as jnp
from jax import lax
from jax.experimental import pallas as pl
from jax.experimental.pallas import tpu as pltpu
from jax.sharding import PartitionSpec as P

highest = lax.Precision.HIGHEST
LANES = 128
COST_SHARE = 8
VMEM_BYTES = 63 * 1024 * 1024
NN = (((1,), (0,)), ((), ()))
NT = (((1,), (1,)), ((), ()))


def round_up(value, step):
    return -(-value // step) * step


def from_behind(block, axis, distance):
    devices = range(lax.axis_size(axis))
    route = [(i - distance, i) for i in devices if i - distance in devices]
    return lax.ppermute(block, axis, route)


def sine(x):
    square = x * x
    tail = 1.0
    for divisor in (156, 110, 72, 42, 20, 6):
        tail = 1.0 - square * (tail * (1.0 / divisor))
    return x * tail


def wave_rows(slots, lons):
    shape = (slots.shape[0], lons)
    lon = lax.broadcasted_iota(jnp.int32, shape, 1)
    part = lax.broadcasted_iota(jnp.int32, shape, 0) % 2
    phase = (slots * lon - part * (lons // 4)).astype(jnp.float32)
    phase = phase - jnp.floor(phase * (1.0 / lons)) * lons
    half = sine((phase - lons / 2) * (math.pi / lons))
    return (2.0 * half * half - 1.0) * math.sqrt(2.0 / lons)


def halves(x):
    upper = x.astype(jnp.bfloat16)
    return upper, (x - upper.astype(jnp.float32)).astype(jnp.bfloat16)


def mxu(a, b, dims):
    return lax.dot_general(a, b, dims, preferred_element_type=jnp.float32)


def dot3(a, b, dims=NN):
    (a_up, a_low), (b_up, b_low) = a, b
    return mxu(a_up, b_up, dims) + (mxu(a_up, b_low, dims) + mxu(a_low, b_up, dims))


def anywhere(arrays):
    return [pl.BlockSpec(memory_space=pl.ANY)] * len(arrays)


def behind(kernel, inputs, after):
    def body(*refs):
        kernel(*refs[:inputs], *refs[inputs + after :])

    return body


MARK = jax.ShapeDtypeStruct((8, LANES), jnp.float32)
MARK_SPEC = pl.BlockSpec(MARK.shape, lambda *_: (0, 0))


def cost(flops):
    return pl.CostEstimate(flops=flops // COST_SHARE, bytes_accessed=0, transcendentals=0)


def gate(block, *after):
    return pl.pallas_call(
        lambda *refs: None,
        in_specs=anywhere((block, *after)),
        out_specs=pl.BlockSpec(memory_space=pl.ANY),
        out_shape=jax.ShapeDtypeStruct(block.shape, block.dtype),
        input_output_aliases={0: 0},
        cost_estimate=pl.CostEstimate(flops=0, bytes_accessed=0, transcendentals=0),
        name="gate",
    )(block, *after)


class Rows:
    def __init__(self, lats, levels, units):
        self.levels, self.units = levels, units
        self.full = lats * levels // LANES * LANES
        self.tail = lats * levels - self.full
        self.lanes = units * self.full + round_up(units * self.tail, LANES)

    def end(self, unit):
        return self.units * self.full + unit * self.tail

    def pieces(self, unit, lat):
        first, last = lat * self.levels, (lat + 1) * self.levels
        pieces = []
        if first < self.full:
            stop = min(last, self.full)
            pieces.append((slice(unit * self.full + first, unit * self.full + stop), slice(0, stop - first)))
        if last > self.full:
            start = max(first, self.full)
            lane = self.end(unit) + start - self.full
            pieces.append((slice(lane, lane + last - start), slice(start - first, self.levels)))
        return pieces


def dft_kernel(steps, place, slot_ref, grad_ref, out_ref, wave_ref, mark_ref, rows_ref):
    mark_ref[...] = jnp.zeros(mark_ref.shape, jnp.float32)
    levels, lats, lons = grad_ref.shape
    waves = wave_ref.shape[0]
    lead = rows_ref.shape[1] // lats

    @pl.when(pl.program_id(0) == 0)
    def _():
        for unit in range(place.units):
            at = slice(unit * LANES, (unit + 1) * LANES)
            wave_ref[at, :lons], wave_ref[at, lons:] = halves(wave_rows(slot_ref[at, :], lons))

    grad = grad_ref[...].reshape(levels * lats, lons)
    terms = mxu(grad, jnp.concatenate([wave_ref[:, :lons], wave_ref[:, lons:]], axis=0), NT)
    coef = terms[:, :waves] + terms[:, waves:]
    for unit in range(place.units):
        rows_ref[unit, 0 : levels * lats, :] = coef[:, unit * LANES : (unit + 1) * LANES]
        if lead > levels:
            rows_ref[unit, levels * lats :, :] = jnp.zeros(((lead - levels) * lats, LANES), jnp.float32)

    for step in range(steps):

        @pl.when(pl.program_id(0) == step)
        def _(step=step):
            if step == 0:
                end = place.end(place.units)
                out_ref[:, end:] = jnp.zeros((LANES, place.lanes - end), jnp.float32)
            for unit in range(place.units):
                for lat in range(lats):
                    part = rows_ref[unit, pl.ds(lat, lead, stride=lats), :].T
                    for lanes, chosen in place.pieces(unit, step * lats + lat):
                        out_ref[:, lanes] = part[:, chosen]


def forward_dft(slots, grad, place, after):
    levels, lats, lons = grad.shape
    waves = slots.shape[0]
    block = 16
    steps = lats // block
    lead = round_up(levels, 8)
    return pl.pallas_call(
        behind(functools.partial(dft_kernel, steps, place), 2, len(after)),
        grid=(steps,),
        in_specs=[
            pl.BlockSpec(slots.shape, lambda i: (0, 0)),
            pl.BlockSpec((levels, block, lons), lambda i: (0, i, 0)),
            *anywhere(after),
        ],
        out_specs=[
            pl.BlockSpec((LANES, place.lanes), lambda i: (0, 0)),
            pl.BlockSpec((waves, 2 * lons), lambda i: (0, 0)),
            MARK_SPEC,
        ],
        out_shape=[
            jax.ShapeDtypeStruct((LANES, place.lanes), jnp.float32),
            jax.ShapeDtypeStruct((waves, 2 * lons), jnp.bfloat16),
            MARK,
        ],
        scratch_shapes=[pltpu.VMEM((place.units, lead * block, LANES), jnp.float32)],
        compiler_params=pltpu.CompilerParams(vmem_limit_bytes=VMEM_BYTES),
        cost_estimate=cost(4 * levels * lats * lons * waves),
        name="forward_dft",
    )(slots, grad, *after)


def spectral_kernel(place, got_ref, end_ref, leg_ref, mat_ref, own_ref, send_ref, flat_ref, cols_ref):
    devices, rows, width = got_ref.shape
    slots, lat_count, _ = leg_ref.shape
    lats = lat_count // devices
    lead = mat_ref.shape[1] // 2
    levels = place.levels
    tiles = width // LANES
    cols_ref[...] = jnp.zeros(cols_ref.shape, jnp.float32)
    for tile in range(tiles):
        piece = got_ref[:, :, tile * LANES : (tile + 1) * LANES]
        flat_ref[tile] = piece.reshape(devices * rows, LANES)
    flat_ref[tiles] = end_ref[...].reshape(devices * rows, LANES)
    mat = halves(mat_ref[...])
    for slot in range(slots):
        turned = []
        for part in range(2):
            row = 2 * slot + part
            lines = [flat_ref[t, pl.ds(row, devices, stride=rows), :] for t in range(tiles + 1)]
            end = place.end(place.unit) % LANES
            lines[tiles] = lines[tiles][:, end : end + place.tail]
            line = jnp.concatenate(lines, axis=1)
            for lat in range(lats):
                cols_ref[pl.ds(row * lat_count + lat, devices, stride=lats), 0:levels] = line[
                    :, lat * levels : (lat + 1) * levels
                ]
            turned.append(cols_ref[row * lat_count : (row + 1) * lat_count, :].T[:lead])
        coef = dot3(halves(jnp.concatenate(turned, axis=0)), halves(leg_ref[slot]))
        mixed = dot3(mat, halves(coef))
        own_ref[slot] = mixed[: 2 * lead]
        send_ref[slot] = mixed[2 * lead :]


def spectral(got, place, unit, legendre, first, mat, after):
    devices, rows, _ = got.shape
    _, lat_count, degrees = legendre.shape
    slots = rows // 2
    lead = mat.shape[1]
    place = copy.copy(place)
    place.unit = unit
    end_tile = place.end(unit) // LANES
    shape = jax.ShapeDtypeStruct((slots, lead, degrees), jnp.float32)
    spec = pl.BlockSpec(shape.shape, lambda i: (0, 0, 0))
    return pl.pallas_call(
        behind(functools.partial(spectral_kernel, place), 4, len(after)),
        grid=(1,),
        in_specs=[
            pl.BlockSpec((devices, rows, place.full), lambda i: (0, 0, unit)),
            pl.BlockSpec((devices, rows, LANES), lambda i: (0, 0, end_tile)),
            pl.BlockSpec((slots, lat_count, degrees), lambda i: (first, 0, 0)),
            pl.BlockSpec(mat.shape, lambda i: (0, 0)),
            *anywhere(after),
        ],
        out_specs=[spec, spec],
        out_shape=[shape, shape],
        scratch_shapes=[
            pltpu.VMEM((place.full // LANES + 1, devices * rows, LANES), jnp.float32),
            pltpu.VMEM((rows * lat_count, LANES), jnp.float32),
        ],
        compiler_params=pltpu.CompilerParams(vmem_limit_bytes=VMEM_BYTES),
        cost_estimate=cost(12 * slots * lat_count * degrees * lead),
        name="spectral_adjoint",
    )(got, got, legendre, mat, *after)


def update_kernel(step_ref, own_ref, got_ref, control_ref, mode_ref, mat_ref, new_ref, keep_ref, send_ref):
    lead = own_ref.shape[1]
    mode = halves(mode_ref[...])
    mat = halves(mat_ref[...])
    for slot in range(own_ref.shape[0]):
        adjoint = dot3(mode, halves(own_ref[slot] + got_ref[slot]))
        control = control_ref[slot]
        new = control - step_ref[0] * (control + adjoint)
        new_ref[slot] = new
        mixed = dot3(mat, halves(new))
        keep_ref[slot] = mixed[:lead]
        send_ref[slot] = mixed[lead:]


def update(step_size, own, got, control, first, mode, mat, after):
    slots, lead, degrees = own.shape
    spec = pl.BlockSpec(own.shape, lambda i: (0, 0, 0))
    shape = jax.ShapeDtypeStruct(own.shape, jnp.float32)
    return pl.pallas_call(
        behind(update_kernel, 6, len(after)),
        grid=(1,),
        in_specs=[
            pl.BlockSpec(memory_space=pltpu.SMEM),
            spec,
            spec,
            pl.BlockSpec(own.shape, lambda i: (first, 0, 0)),
            pl.BlockSpec(mode.shape, lambda i: (0, 0)),
            pl.BlockSpec(mat.shape, lambda i: (0, 0)),
            *anywhere(after),
        ],
        out_specs=[spec, spec, spec],
        out_shape=[shape, shape, shape],
        compiler_params=pltpu.CompilerParams(vmem_limit_bytes=VMEM_BYTES),
        cost_estimate=cost(36 * slots * lead * lead * degrees),
        name="gradient_step",
    )(step_size, own, got, control, mode, mat, *after)


def back_kernel(place, *refs):
    units = place.units
    keep_refs, got_refs = refs[:units], refs[units : 2 * units]
    leg_ref, mat_ref, out_ref, mark_ref, cols_ref, line_ref, flat_ref = refs[2 * units :]
    mark_ref[...] = jnp.zeros(mark_ref.shape, jnp.float32)
    devices, rows, _ = out_ref.shape
    slots, lat_count, degrees = leg_ref.shape
    lats = lat_count // devices
    lead = mat_ref.shape[0] // 2
    levels = place.levels
    tiles = place.full // LANES
    mat = halves(mat_ref[...])
    gap = jnp.zeros((LANES - lead, degrees), jnp.float32)

    for unit in range(units):

        @pl.when(pl.program_id(0) == unit)
        def _(unit=unit):
            if unit == 0:
                out_ref[:, :, units * place.full :] = jnp.zeros(
                    (devices, rows, place.lanes - units * place.full), jnp.float32
                )
            if place.tail:
                unused = (line_ref.shape[0], LANES - place.tail)
                line_ref[:, place.full + place.tail :] = jnp.zeros(unused, jnp.float32)
            for slot in range(slots):
                coef = dot3(mat, halves(keep_refs[unit][slot] + got_refs[unit][slot]))
                coef = jnp.concatenate([coef[:lead], gap, coef[lead:], gap], axis=0)
                fourier = dot3(halves(leg_ref[slot]), halves(coef), NT)
                for part in range(2):
                    row = 2 * slot + part
                    base = row * lat_count
                    cols_ref[base : base + lat_count, :] = fourier[:, part * LANES : (part + 1) * LANES]
                    line = slice(row * devices, (row + 1) * devices)
                    for lat in range(lats):
                        piece = cols_ref[pl.ds(base + lat, devices, stride=lats), :]
                        line_ref[line, lat * levels : (lat + 1) * levels] = piece[:, :levels]
                    for tile in range(line_ref.shape[1] // LANES):
                        flat_ref[tile, pl.ds(row, devices, stride=rows), :] = line_ref[
                            line, tile * LANES : (tile + 1) * LANES
                        ]
            for tile in range(tiles):
                start = unit * place.full + tile * LANES
                out_ref[:, :, start : start + LANES] = flat_ref[tile].reshape(devices, rows, LANES)
            if place.tail:
                lane = place.end(unit)
                ends = flat_ref[tiles].reshape(devices, rows, LANES)[:, :, : place.tail]
                out_ref[:, :, lane : lane + place.tail] = ends


def spectral_back(keeps, gots, place, legendre, first, mat, devices, after):
    slots, lead, degrees = keeps[0].shape
    lat_count = legendre.shape[1]
    rows = 2 * slots
    units = place.units
    spec = pl.BlockSpec(keeps[0].shape, lambda i: (0, 0, 0))
    padded_row = place.full + (LANES if place.tail else 0)
    shape = jax.ShapeDtypeStruct((devices, rows, place.lanes), jnp.float32)
    return pl.pallas_call(
        behind(functools.partial(back_kernel, place), 2 * units + 2, len(after)),
        grid=(units,),
        in_specs=[spec] * (2 * units)
        + [
            pl.BlockSpec((slots, lat_count, degrees), lambda i: (i + first, 0, 0)),
            pl.BlockSpec(mat.shape, lambda i: (0, 0)),
            *anywhere(after),
        ],
        out_specs=[pl.BlockSpec(shape.shape, lambda i: (0, 0, 0)), MARK_SPEC],
        out_shape=[shape, MARK],
        scratch_shapes=[
            pltpu.VMEM((rows * lat_count, LANES), jnp.float32),
            pltpu.VMEM((rows * devices, padded_row), jnp.float32),
            pltpu.VMEM((padded_row // LANES, devices * rows, LANES), jnp.float32),
        ],
        compiler_params=pltpu.CompilerParams(vmem_limit_bytes=VMEM_BYTES),
        cost_estimate=cost(12 * units * slots * lat_count * degrees * lead),
        name="spectral_forward",
    )(*keeps, *gots, legendre, mat, *after)


def inverse_kernel(steps, place, has_total, coef_ref, up_ref, low_ref, *refs):
    total_ref = refs[0] if has_total else None
    out_ref, rows_ref, left_ref = refs[has_total:]
    levels, lats, columns = out_ref.shape
    waves = up_ref.shape[0]

    for step in range(steps):

        @pl.when(pl.program_id(0) == step)
        def _(step=step):
            for unit in range(place.units):
                for lat in range(lats):
                    parts = [coef_ref[:, at] for at, _ in place.pieces(unit, step * lats + lat)]
                    part = parts[0] if len(parts) == 1 else jnp.concatenate(parts, axis=1)
                    rows_ref[unit, pl.ds(lat, levels, stride=lats), :] = part.T
                high, rest = halves(rows_ref[unit])
                for term, value in enumerate((high, rest, high)):
                    start = term * waves + unit * LANES
                    left_ref[:, start : start + LANES] = value

    width = 512 if columns % 512 == 0 else columns
    for first in range(0, columns, width):
        at = slice(first, first + width)
        right = jnp.concatenate([up_ref[:, at], up_ref[:, at], low_ref[:, at]], axis=0)
        result = mxu(left_ref[...], right, NN).reshape(levels, lats, width)
        if has_total:
            result = result + total_ref[:, :, at]
        out_ref[:, :, at] = result.astype(out_ref.dtype)


def inverse_dft(coef, place, table, total, lats, dtype, after):
    waves = table.shape[0]
    lons = table.shape[1] // 2
    levels = place.levels
    block = 16
    steps = lats // block
    grid_spec = pl.BlockSpec((levels, block, lons), lambda i: (0, i, 0))
    totals = [] if total is None else [total]
    return pl.pallas_call(
        behind(functools.partial(inverse_kernel, steps, place, len(totals)), 3 + len(totals), len(after)),
        grid=(steps,),
        in_specs=[
            pl.BlockSpec(coef.shape, lambda i: (0, 0)),
            pl.BlockSpec((waves, lons), lambda i: (0, 0)),
            pl.BlockSpec((waves, lons), lambda i: (0, 1)),
        ]
        + [grid_spec] * len(totals)
        + anywhere(after),
        out_specs=grid_spec,
        out_shape=jax.ShapeDtypeStruct((levels, lats, lons), dtype),
        scratch_shapes=[
            pltpu.VMEM((place.units, levels * block, LANES), jnp.float32),
            pltpu.VMEM((levels * block, 3 * waves), jnp.bfloat16),
        ],
        compiler_params=pltpu.CompilerParams(vmem_limit_bytes=VMEM_BYTES),
        cost_estimate=cost(6 * levels * lats * lons * waves),
        name="inverse_dft",
    )(coef, table, table, *totals, *after)


def padded(matrix, lead):
    return jnp.pad(matrix, ((0, lead - matrix.shape[0]), (0, lead - matrix.shape[1])))


def on_both(matrix, lead):
    return jnp.kron(jnp.eye(2, dtype=jnp.float32), padded(matrix, lead))


def exchange(block):
    return lax.all_to_all(block, "lat", split_axis=0, concat_axis=0, tiled=True)


def tiled_local(grad_grid, remap, modes, balance, legendre, control, step_size, owner_slots):
    _, lats, levels, lons = grad_grid.shape
    owned, _, degrees = legendre.shape
    wave_count = owner_slots.shape[0]
    devices = wave_count // owned
    lead = round_up(levels, 8)
    grad = jnp.transpose(grad_grid[0], (1, 0, 2))
    units = owned // 4
    sizes = [1, units - 3, 2] if units > 3 else [units]
    place = [Rows(lats, levels, size) for size in sizes]
    members, first = [], 0
    for size in sizes:
        members.append(list(range(first, first + size)))
        first += size
    by_owner = owner_slots.reshape(devices, units, 4).transpose(1, 0, 2)

    row_slots = jnp.repeat(by_owner.reshape(units * LANES // 2), 2)[:, None]
    waves = {}
    mix = functools.partial(jnp.einsum, precision=highest)
    adjoint_mat = jnp.concatenate(
        [on_both(remap[0].T, lead), on_both(mix("ik,kj->ji", remap[0], balance), lead)]
    )
    mode_mat = on_both(modes[0].T, lead)
    forward_mat = jnp.concatenate(
        [on_both(modes[0], lead), on_both(mix("ik,kj->ij", balance, modes[0]), lead)]
    )
    remap_mat = on_both(remap[0], lead)
    own_control = control[0].reshape(owned, 2, levels, degrees)
    own_control = jnp.pad(own_control, ((0, 0), (0, 0), (0, lead - levels), (0, 0)))
    own_control = own_control.reshape(owned, 2 * lead, degrees)
    own, send, other, new, keep, back_send, back_other = ({} for _ in range(7))

    def dft(c, *after):
        rows = slice(members[c][0] * LANES, (members[c][-1] + 1) * LANES)
        coef, waves[c], mark = forward_dft(row_slots[rows], grad, place[c], after)
        return coef.reshape(devices, 8, place[c].lanes), mark

    def adjoint(c, got, *after):
        for at, u in enumerate(members[c]):
            own[u], send[u] = spectral(got, place[c], at, legendre, u, adjoint_mat, after)
            other[u] = from_behind(send[u], "var", -1)
            after = (own[u],)

    def gradient_step(group, *after):
        for u in group:
            new[u], keep[u], back_send[u] = update(
                step_size, own[u], other[u], own_control, u, mode_mat, forward_mat, after
            )
            after = (new[u],)
            back_other[u] = from_behind(back_send[u], "var", 1)

    def forward(group, *after):
        keeps, gots = [keep[u] for u in group], [back_other[u] for u in group]
        at = Rows(lats, levels, len(group))
        return spectral_back(keeps, gots, at, legendre, group[0], remap_mat, devices, after)

    def inverse(group, arrived, total, dtype, *after):
        at = Rows(lats, levels, len(group))
        rows = []
        for c, chunk in enumerate(members):
            shared = [u - chunk[0] for u in group if u in chunk]
            if shared:
                rows.append(waves[c][shared[0] * LANES : (shared[-1] + 1) * LANES])
        coef = arrived.reshape(LANES, at.lanes)
        return inverse_dft(coef, at, jnp.concatenate(rows), total, lats, dtype, after)

    def all_new():
        updated = jnp.concatenate([new[u] for u in range(units)]).reshape(owned, 2, lead, degrees)
        return updated[:, :, :levels].reshape(owned, 2 * levels, degrees)

    if len(sizes) == 3:
        coef_a, _ = dft(0)
        got_a = exchange(coef_a)
        coef_b, _ = dft(1)
        got_b = exchange(gate(coef_b, got_a))
        coef_c, _ = dft(2, got_a)
        adjoint(0, got_a)
        gradient_step(members[0])
        got_c = exchange(gate(coef_c, got_b, back_other[0]))
        adjoint(1, got_b)
        gradient_step(members[1][:-1])
        early, middle, late = members[0] + members[1][:1], members[1][1:] + members[2][:1], members[2][1:]
        back_a, mark = forward(early)
        gradient_step(members[1][-1:], mark)
        arrived_a = exchange(gate(back_a, got_c, back_other[members[1][-2]], other[members[1][-1]]))
        adjoint(2, got_c)
        gradient_step(members[2])
        back_b, _ = forward(middle)
        arrived_b = exchange(gate(back_b, arrived_a, own[members[2][-1]]))
        back_c, _ = forward(late)
        total = inverse(early, arrived_a, None, jnp.float32)
        arrived_c = exchange(gate(back_c, arrived_b, total))
        updated = all_new()
        total = inverse(middle, arrived_b, total, jnp.float32)
        total = inverse(late, arrived_c, total, jnp.bfloat16)
    else:
        coef, _ = dft(0)
        adjoint(0, exchange(coef))
        gradient_step(members[0])
        updated = all_new()
        back, _ = forward(members[0])
        total = inverse(members[0], exchange(back), None, jnp.bfloat16)
    increment = jnp.transpose(total, (1, 0, 2))
    return (updated[None], increment[None])


def make_waves(owner_slots, lon_count):
    longitude = lax.iota(jnp.int32, lon_count)
    phases = longitude[:, None] * owner_slots[None, :] % lon_count
    angles = phases.astype(jnp.float32) * (2.0 * math.pi / lon_count)
    factor = math.sqrt(2.0 / lon_count)
    return jnp.stack([jnp.cos(angles), jnp.sin(angles)], axis=1) * factor


def plain_local(grad_grid, remap, modes, balance, legendre, control, step_size, owner_slots):
    lat_rows = grad_grid.shape[1]
    levels = grad_grid.shape[2]
    lon_count = grad_grid.shape[3]
    wave_count = owner_slots.shape[0]
    owned_count = legendre.shape[0]
    degrees = legendre.shape[2]
    wave_table = make_waves(owner_slots, lon_count)
    remap_var = remap[0]
    modes_var = modes[0]
    lifted = jnp.einsum(
        "ik,lij->lkj", remap_var, grad_grid[0].astype(jnp.float32), precision=highest
    )
    slab_coef = jnp.einsum("lkj,jcs->slck", lifted, wave_table, precision=highest)
    spectral_coef = jnp.einsum(
        "sln,slq->sqn",
        legendre,
        lax.all_to_all(
            slab_coef.reshape(wave_count, lat_rows, 2 * levels),
            "lat",
            split_axis=0,
            concat_axis=1,
            tiled=True,
        ),
        precision=highest,
    )
    spec_four = spectral_coef.reshape(owned_count, 2, levels, degrees)
    partner = from_behind(spec_four, "var", -1)
    blended = spec_four + jnp.einsum("ik,scin->sckn", balance, partner, precision=highest)
    spectral_coef = jnp.einsum("ik,scin->sckn", modes_var, blended, precision=highest).reshape(
        owned_count, 2 * levels, degrees
    )
    own_control = control[0]
    updated = own_control - step_size[0] * (own_control + spectral_coef)
    level_coef = jnp.einsum(
        "ki,scin->sckn",
        modes_var,
        updated.reshape(owned_count, 2, levels, degrees),
        precision=highest,
    )
    partner = from_behind(level_coef, "var", 1)
    level_coef = level_coef + jnp.einsum("ki,scin->sckn", balance, partner, precision=highest)
    level_coef = level_coef.reshape(owned_count, 2 * levels, degrees)
    fourier = jnp.einsum("sln,sqn->slq", legendre, level_coef, precision=highest)
    slab_back = lax.all_to_all(fourier, "lat", split_axis=1, concat_axis=0, tiled=True)
    slab_back = slab_back.reshape(wave_count, lat_rows, 2, levels)
    lowered = jnp.einsum("slck,jcs->lkj", slab_back, wave_table, precision=highest)
    increment = jnp.einsum("ik,lkj->lij", remap_var, lowered, precision=highest).astype(
        jnp.bfloat16
    )
    return (updated[None], increment[None])


def local(*arrays):
    grad_grid, legendre = arrays[0], arrays[4]
    devices = legendre.shape[1] // grad_grid.shape[1]
    levels = grad_grid.shape[2]
    tail = grad_grid.shape[1] * levels % LANES
    fits = (
        legendre.shape[0] % 4 == 0
        and grad_grid.shape[1] % 16 == 0
        and devices * 8 == LANES
        and round_up(levels, 8) <= LANES
        and tail > 0
        and grad_grid.shape[3] % 4 == 0
        and LANES % tail == 0
    )
    return (tiled_local if fits else plain_local)(*arrays)


def solution(mesh):
    return jax.shard_map(
        local,
        mesh=mesh,
        in_specs=(
            P("var", "lat", None, None),
            P("var", None, None),
            P("var", None, None),
            P(),
            P("lat", None, None),
            P("var", "lat", None, None),
            P("var"),
            P(),
        ),
        out_specs=(P("var", "lat", None, None), P("var", "lat", None, None)),
        check_vma=False,
    )
```

```python
import copy
import functools
import math

import jax
import jax.numpy as jnp
from jax import lax
from jax.experimental import pallas as pl
from jax.experimental.pallas import tpu as pltpu
from jax.sharding import PartitionSpec as P

highest = lax.Precision.HIGHEST
LANES = 128
COST_SHARE = 8
VMEM_BYTES = 63 * 1024 * 1024
NN = (((1,), (0,)), ((), ()))
NT = (((1,), (1,)), ((), ()))


def round_up(value, step):
    return -(-value // step) * step


def from_behind(block, axis, distance):
    devices = range(lax.axis_size(axis))
    route = [(i - distance, i) for i in devices if i - distance in devices]
    return lax.ppermute(block, axis, route)


def sine(x):
    square = x * x
    tail = 1.0
    for divisor in (156, 110, 72, 42, 20, 6):
        tail = 1.0 - square * (tail * (1.0 / divisor))
    return x * tail


def wave_rows(slots, lons):
    shape = (slots.shape[0], lons)
    lon = lax.broadcasted_iota(jnp.int32, shape, 1)
    part = lax.broadcasted_iota(jnp.int32, shape, 0) % 2
    phase = (slots * lon - part * (lons // 4)).astype(jnp.float32)
    phase = phase - jnp.floor(phase * (1.0 / lons)) * lons
    half = sine((phase - lons / 2) * (math.pi / lons))
    return (2.0 * half * half - 1.0) * math.sqrt(2.0 / lons)


def halves(x):
    upper = x.astype(jnp.bfloat16)
    return upper, (x - upper.astype(jnp.float32)).astype(jnp.bfloat16)


def mxu(a, b, dims):
    return lax.dot_general(a, b, dims, preferred_element_type=jnp.float32)


def dot3(a, b, dims=NN):
    (a_up, a_low), (b_up, b_low) = a, b
    return mxu(a_up, b_up, dims) + (mxu(a_up, b_low, dims) + mxu(a_low, b_up, dims))


def anywhere(arrays):
    return [pl.BlockSpec(memory_space=pl.ANY)] * len(arrays)


def behind(kernel, inputs, after):
    def body(*refs):
        kernel(*refs[:inputs], *refs[inputs + after :])

    return body


MARK = jax.ShapeDtypeStruct((8, LANES), jnp.float32)
MARK_SPEC = pl.BlockSpec(MARK.shape, lambda *_: (0, 0))


def cost(flops):
    return pl.CostEstimate(flops=flops // COST_SHARE, bytes_accessed=0, transcendentals=0)


def gate(block, *after):
    return pl.pallas_call(
        lambda *refs: None,
        in_specs=anywhere((block, *after)),
        out_specs=pl.BlockSpec(memory_space=pl.ANY),
        out_shape=jax.ShapeDtypeStruct(block.shape, block.dtype),
        input_output_aliases={0: 0},
        cost_estimate=pl.CostEstimate(flops=0, bytes_accessed=0, transcendentals=0),
        name="gate",
    )(block, *after)


class Rows:
    def __init__(self, lats, levels, units):
        self.levels, self.units = levels, units
        self.full = lats * levels // LANES * LANES
        self.tail = lats * levels - self.full
        self.lanes = units * self.full + round_up(units * self.tail, LANES)

    def end(self, unit):
        return self.units * self.full + unit * self.tail

    def pieces(self, unit, lat):
        first, last = lat * self.levels, (lat + 1) * self.levels
        pieces = []
        if first < self.full:
            stop = min(last, self.full)
            pieces.append((slice(unit * self.full + first, unit * self.full + stop), slice(0, stop - first)))
        if last > self.full:
            start = max(first, self.full)
            lane = self.end(unit) + start - self.full
            pieces.append((slice(lane, lane + last - start), slice(start - first, self.levels)))
        return pieces


def dft_kernel(steps, place, slot_ref, grad_ref, out_ref, wave_ref, mark_ref, rows_ref, right_ref):
    mark_ref[...] = jnp.zeros(mark_ref.shape, jnp.float32)
    levels, lats, lons = grad_ref.shape
    waves = wave_ref.shape[0]
    lead = rows_ref.shape[1] // lats

    @pl.when(pl.program_id(0) == 0)
    def _():
        for unit in range(place.units):
            at = slice(unit * LANES, (unit + 1) * LANES)
            rows = wave_rows(slot_ref[at, :], lons)
            wave_ref[at, :lons], wave_ref[at, lons:] = halves(rows)
            high, rest = halves(rows.T)
            right_ref[:, at] = high
            right_ref[:, waves + unit * LANES : waves + (unit + 1) * LANES] = rest

    grad = grad_ref[...].reshape(levels * lats, lons)
    terms = mxu(grad, right_ref[...], NN)
    coef = terms[:, :waves] + terms[:, waves:]
    for unit in range(place.units):
        rows_ref[unit, 0 : levels * lats, :] = coef[:, unit * LANES : (unit + 1) * LANES]
        if lead > levels:
            rows_ref[unit, levels * lats :, :] = jnp.zeros(((lead - levels) * lats, LANES), jnp.float32)

    for step in range(steps):

        @pl.when(pl.program_id(0) == step)
        def _(step=step):
            if step == 0:
                end = place.end(place.units)
                out_ref[:, end:] = jnp.zeros((LANES, place.lanes - end), jnp.float32)
            for unit in range(place.units):
                for lat in range(lats):
                    part = rows_ref[unit, pl.ds(lat, lead, stride=lats), :].T
                    for lanes, chosen in place.pieces(unit, step * lats + lat):
                        out_ref[:, lanes] = part[:, chosen]


def forward_dft(slots, grad, place, after):
    levels, lats, lons = grad.shape
    waves = slots.shape[0]
    block = 16
    steps = lats // block
    lead = round_up(levels, 8)
    return pl.pallas_call(
        behind(functools.partial(dft_kernel, steps, place), 2, len(after)),
        grid=(steps,),
        in_specs=[
            pl.BlockSpec(slots.shape, lambda i: (0, 0)),
            pl.BlockSpec((levels, block, lons), lambda i: (0, i, 0)),
            *anywhere(after),
        ],
        out_specs=[
            pl.BlockSpec((LANES, place.lanes), lambda i: (0, 0)),
            pl.BlockSpec((waves, 2 * lons), lambda i: (0, 0)),
            MARK_SPEC,
        ],
        out_shape=[
            jax.ShapeDtypeStruct((LANES, place.lanes), jnp.float32),
            jax.ShapeDtypeStruct((waves, 2 * lons), jnp.bfloat16),
            MARK,
        ],
        scratch_shapes=[
            pltpu.VMEM((place.units, lead * block, LANES), jnp.float32),
            pltpu.VMEM((lons, 2 * waves), jnp.bfloat16),
        ],
        compiler_params=pltpu.CompilerParams(vmem_limit_bytes=VMEM_BYTES),
        cost_estimate=cost(4 * levels * lats * lons * waves),
        name="forward_dft",
    )(slots, grad, *after)


def spectral_kernel(place, got_ref, end_ref, leg_ref, mat_ref, own_ref, send_ref, flat_ref, cols_ref):
    devices, rows, width = got_ref.shape
    slots, lat_count, _ = leg_ref.shape
    lats = lat_count // devices
    lead = mat_ref.shape[1] // 2
    levels = place.levels
    tiles = width // LANES
    cols_ref[...] = jnp.zeros(cols_ref.shape, jnp.float32)
    for tile in range(tiles):
        piece = got_ref[:, :, tile * LANES : (tile + 1) * LANES]
        flat_ref[tile] = piece.reshape(devices * rows, LANES)
    flat_ref[tiles] = end_ref[...].reshape(devices * rows, LANES)
    mat = halves(mat_ref[...])
    for slot in range(slots):
        turned = []
        for part in range(2):
            row = 2 * slot + part
            lines = [flat_ref[t, pl.ds(row, devices, stride=rows), :] for t in range(tiles + 1)]
            end = place.end(place.unit) % LANES
            lines[tiles] = lines[tiles][:, end : end + place.tail]
            line = jnp.concatenate(lines, axis=1)
            for lat in range(lats):
                cols_ref[pl.ds(row * lat_count + lat, devices, stride=lats), 0:levels] = line[
                    :, lat * levels : (lat + 1) * levels
                ]
            turned.append(cols_ref[row * lat_count : (row + 1) * lat_count, :].T[:lead])
        coef = dot3(halves(jnp.concatenate(turned, axis=0)), halves(leg_ref[slot]))
        mixed = dot3(mat, halves(coef))
        own_ref[slot] = mixed[: 2 * lead]
        send_ref[slot] = mixed[2 * lead :]


def spectral(got, place, unit, legendre, first, mat, after):
    devices, rows, _ = got.shape
    _, lat_count, degrees = legendre.shape
    slots = rows // 2
    lead = mat.shape[1]
    place = copy.copy(place)
    place.unit = unit
    end_tile = place.end(unit) // LANES
    shape = jax.ShapeDtypeStruct((slots, lead, degrees), jnp.float32)
    spec = pl.BlockSpec(shape.shape, lambda i: (0, 0, 0))
    return pl.pallas_call(
        behind(functools.partial(spectral_kernel, place), 4, len(after)),
        grid=(1,),
        in_specs=[
            pl.BlockSpec((devices, rows, place.full), lambda i: (0, 0, unit)),
            pl.BlockSpec((devices, rows, LANES), lambda i: (0, 0, end_tile)),
            pl.BlockSpec((slots, lat_count, degrees), lambda i: (first, 0, 0)),
            pl.BlockSpec(mat.shape, lambda i: (0, 0)),
            *anywhere(after),
        ],
        out_specs=[spec, spec],
        out_shape=[shape, shape],
        scratch_shapes=[
            pltpu.VMEM((place.full // LANES + 1, devices * rows, LANES), jnp.float32),
            pltpu.VMEM((rows * lat_count, LANES), jnp.float32),
        ],
        compiler_params=pltpu.CompilerParams(vmem_limit_bytes=VMEM_BYTES),
        cost_estimate=cost(12 * slots * lat_count * degrees * lead),
        name="spectral_adjoint",
    )(got, got, legendre, mat, *after)


def update_kernel(step_ref, own_ref, got_ref, control_ref, mode_ref, mat_ref, new_ref, keep_ref, send_ref):
    lead = own_ref.shape[1]
    mode = halves(mode_ref[...])
    mat = halves(mat_ref[...])
    for slot in range(own_ref.shape[0]):
        adjoint = dot3(mode, halves(own_ref[slot] + got_ref[slot]))
        control = control_ref[slot]
        new = control - step_ref[0] * (control + adjoint)
        new_ref[slot] = new
        mixed = dot3(mat, halves(new))
        keep_ref[slot] = mixed[:lead]
        send_ref[slot] = mixed[lead:]


def update(step_size, own, got, control, first, mode, mat, after):
    slots, lead, degrees = own.shape
    spec = pl.BlockSpec(own.shape, lambda i: (0, 0, 0))
    shape = jax.ShapeDtypeStruct(own.shape, jnp.float32)
    return pl.pallas_call(
        behind(update_kernel, 6, len(after)),
        grid=(1,),
        in_specs=[
            pl.BlockSpec(memory_space=pltpu.SMEM),
            spec,
            spec,
            pl.BlockSpec(own.shape, lambda i: (first, 0, 0)),
            pl.BlockSpec(mode.shape, lambda i: (0, 0)),
            pl.BlockSpec(mat.shape, lambda i: (0, 0)),
            *anywhere(after),
        ],
        out_specs=[spec, spec, spec],
        out_shape=[shape, shape, shape],
        compiler_params=pltpu.CompilerParams(vmem_limit_bytes=VMEM_BYTES),
        cost_estimate=cost(36 * slots * lead * lead * degrees),
        name="gradient_step",
    )(step_size, own, got, control, mode, mat, *after)


def back_kernel(place, units, skip, *refs):
    keep_refs, got_refs = refs[:units], refs[units : 2 * units]
    leg_ref, mat_ref = refs[2 * units : 2 * units + 2]
    out_ref, mark_ref, cols_ref, line_ref, flat_ref = refs[-5:]
    mark_ref[...] = jnp.zeros(mark_ref.shape, jnp.float32)
    devices, rows, _ = out_ref.shape
    slots, lat_count, degrees = leg_ref.shape
    lats = lat_count // devices
    lead = mat_ref.shape[0] // 2
    levels = place.levels
    tiles = place.full // LANES
    mat = halves(mat_ref[...])
    gap = jnp.zeros((LANES - lead, degrees), jnp.float32)

    for unit in range(units):

        @pl.when(pl.program_id(0) == unit)
        def _(unit=unit):
            if unit == 0 and skip:
                out_ref[...] = refs[2 * units + 2][...]
            elif unit == 0:
                ends = place.units * place.full
                out_ref[:, :, ends:] = jnp.zeros((devices, rows, place.lanes - ends), jnp.float32)
            if place.tail:
                unused = (line_ref.shape[0], LANES - place.tail)
                line_ref[:, place.full + place.tail :] = jnp.zeros(unused, jnp.float32)
            for slot in range(slots):
                coef = dot3(mat, halves(keep_refs[unit][slot] + got_refs[unit][slot]))
                coef = jnp.concatenate([coef[:lead], gap, coef[lead:], gap], axis=0)
                fourier = dot3(halves(leg_ref[slot]), halves(coef), NT)
                for part in range(2):
                    row = 2 * slot + part
                    base = row * lat_count
                    cols_ref[base : base + lat_count, :] = fourier[:, part * LANES : (part + 1) * LANES]
                    line = slice(row * devices, (row + 1) * devices)
                    for lat in range(lats):
                        piece = cols_ref[pl.ds(base + lat, devices, stride=lats), :]
                        line_ref[line, lat * levels : (lat + 1) * levels] = piece[:, :levels]
                    for tile in range(line_ref.shape[1] // LANES):
                        flat_ref[tile, pl.ds(row, devices, stride=rows), :] = line_ref[
                            line, tile * LANES : (tile + 1) * LANES
                        ]
            for tile in range(tiles):
                start = (skip + unit) * place.full + tile * LANES
                out_ref[:, :, start : start + LANES] = flat_ref[tile].reshape(devices, rows, LANES)
            if place.tail:
                lane = place.end(skip + unit)
                ends = flat_ref[tiles].reshape(devices, rows, LANES)[:, :, : place.tail]
                out_ref[:, :, lane : lane + place.tail] = ends


def spectral_back(keeps, gots, place, legendre, first, mat, devices, before, skip, after):
    slots, lead, degrees = keeps[0].shape
    lat_count = legendre.shape[1]
    rows = 2 * slots
    units = len(keeps)
    spec = pl.BlockSpec(keeps[0].shape, lambda i: (0, 0, 0))
    padded_row = place.full + (LANES if place.tail else 0)
    shape = jax.ShapeDtypeStruct((devices, rows, place.lanes), jnp.float32)
    return pl.pallas_call(
        behind(
            functools.partial(back_kernel, place, units, skip), 2 * units + 2 + len(before), len(after)
        ),
        grid=(units,),
        in_specs=[spec] * (2 * units)
        + [
            pl.BlockSpec((slots, lat_count, degrees), lambda i: (i + first, 0, 0)),
            pl.BlockSpec(mat.shape, lambda i: (0, 0)),
            *[pl.BlockSpec(b.shape, lambda i: (0, 0, 0)) for b in before],
            *anywhere(after),
        ],
        out_specs=[pl.BlockSpec(shape.shape, lambda i: (0, 0, 0)), MARK_SPEC],
        out_shape=[shape, MARK],
        scratch_shapes=[
            pltpu.VMEM((rows * lat_count, LANES), jnp.float32),
            pltpu.VMEM((rows * devices, padded_row), jnp.float32),
            pltpu.VMEM((padded_row // LANES, devices * rows, LANES), jnp.float32),
        ],
        compiler_params=pltpu.CompilerParams(vmem_limit_bytes=VMEM_BYTES),
        cost_estimate=cost(12 * units * slots * lat_count * degrees * lead),
        name="spectral_forward",
    )(*keeps, *gots, legendre, mat, *before, *after)


def inverse_kernel(steps, place, has_total, coef_ref, up_ref, low_ref, *refs):
    total_ref = refs[0] if has_total else None
    out_ref, rows_ref, left_ref = refs[has_total:]
    levels, lats, columns = out_ref.shape
    waves = up_ref.shape[0]

    for step in range(steps):

        @pl.when(pl.program_id(0) == step)
        def _(step=step):
            for unit in range(place.units):
                for lat in range(lats):
                    parts = [coef_ref[:, at] for at, _ in place.pieces(unit, step * lats + lat)]
                    part = parts[0] if len(parts) == 1 else jnp.concatenate(parts, axis=1)
                    rows_ref[unit, pl.ds(lat, levels, stride=lats), :] = part.T
                high, rest = halves(rows_ref[unit])
                for term, value in enumerate((high, rest, high)):
                    start = term * waves + unit * LANES
                    left_ref[:, start : start + LANES] = value

    width = 512 if columns % 512 == 0 else columns
    for first in range(0, columns, width):
        at = slice(first, first + width)
        right = jnp.concatenate([up_ref[:, at], up_ref[:, at], low_ref[:, at]], axis=0)
        result = mxu(left_ref[...], right, NN).reshape(levels, lats, width)
        if has_total:
            result = result + total_ref[:, :, at]
        out_ref[:, :, at] = result.astype(out_ref.dtype)


def inverse_dft(coef, place, table, total, lats, dtype, after):
    waves = table.shape[0]
    lons = table.shape[1] // 2
    levels = place.levels
    block = 16
    steps = lats // block
    grid_spec = pl.BlockSpec((levels, block, lons), lambda i: (0, i, 0))
    totals = [] if total is None else [total]
    return pl.pallas_call(
        behind(functools.partial(inverse_kernel, steps, place, len(totals)), 3 + len(totals), len(after)),
        grid=(steps,),
        in_specs=[
            pl.BlockSpec(coef.shape, lambda i: (0, 0)),
            pl.BlockSpec((waves, lons), lambda i: (0, 0)),
            pl.BlockSpec((waves, lons), lambda i: (0, 1)),
        ]
        + [grid_spec] * len(totals)
        + anywhere(after),
        out_specs=grid_spec,
        out_shape=jax.ShapeDtypeStruct((levels, lats, lons), dtype),
        scratch_shapes=[
            pltpu.VMEM((place.units, levels * block, LANES), jnp.float32),
            pltpu.VMEM((levels * block, 3 * waves), jnp.bfloat16),
        ],
        compiler_params=pltpu.CompilerParams(vmem_limit_bytes=VMEM_BYTES),
        cost_estimate=cost(6 * levels * lats * lons * waves),
        name="inverse_dft",
    )(coef, table, table, *totals, *after)


def padded(matrix, lead):
    return jnp.pad(matrix, ((0, lead - matrix.shape[0]), (0, lead - matrix.shape[1])))


def on_both(matrix, lead):
    return jnp.kron(jnp.eye(2, dtype=jnp.float32), padded(matrix, lead))


def exchange(block):
    return lax.all_to_all(block, "lat", split_axis=0, concat_axis=0, tiled=True)


def tiled_local(grad_grid, remap, modes, balance, legendre, control, step_size, owner_slots):
    _, lats, levels, lons = grad_grid.shape
    owned, _, degrees = legendre.shape
    wave_count = owner_slots.shape[0]
    devices = wave_count // owned
    lead = round_up(levels, 8)
    grad = jnp.transpose(grad_grid[0], (1, 0, 2))
    units = owned // 4
    sizes = [1, units - 3, 2] if units > 3 else [units]
    place = [Rows(lats, levels, size) for size in sizes]
    members, first = [], 0
    for size in sizes:
        members.append(list(range(first, first + size)))
        first += size
    by_owner = owner_slots.reshape(devices, units, 4).transpose(1, 0, 2)

    row_slots = jnp.repeat(by_owner.reshape(units * LANES // 2), 2)[:, None]
    waves = {}
    mix = functools.partial(jnp.einsum, precision=highest)
    adjoint_mat = jnp.concatenate(
        [on_both(remap[0].T, lead), on_both(mix("ik,kj->ji", remap[0], balance), lead)]
    )
    mode_mat = on_both(modes[0].T, lead)
    forward_mat = jnp.concatenate(
        [on_both(modes[0], lead), on_both(mix("ik,kj->ij", balance, modes[0]), lead)]
    )
    remap_mat = on_both(remap[0], lead)
    own_control = control[0].reshape(owned, 2, levels, degrees)
    own_control = jnp.pad(own_control, ((0, 0), (0, 0), (0, lead - levels), (0, 0)))
    own_control = own_control.reshape(owned, 2 * lead, degrees)
    own, send, other, new, keep, back_send, back_other = ({} for _ in range(7))

    def dft(c, *after):
        rows = slice(members[c][0] * LANES, (members[c][-1] + 1) * LANES)
        coef, waves[c], mark = forward_dft(row_slots[rows], grad, place[c], after)
        return coef.reshape(devices, 8, place[c].lanes), mark

    def adjoint(c, got, *after):
        for at, u in enumerate(members[c]):
            own[u], send[u] = spectral(got, place[c], at, legendre, u, adjoint_mat, after)
            other[u] = from_behind(send[u], "var", -1)
            after = (own[u],)

    def gradient_step(group, *after):
        for u in group:
            new[u], keep[u], back_send[u] = update(
                step_size, own[u], other[u], own_control, u, mode_mat, forward_mat, after
            )
            after = (new[u],)
            back_other[u] = from_behind(back_send[u], "var", 1)

    def forward(group, parts=1):
        at = Rows(lats, levels, len(group))
        before, skip = [], 0
        for some in [group] if parts == 1 else [group[:-1], group[-1:]]:
            keeps, gots = [keep[u] for u in some], [back_other[u] for u in some]
            back, mark = spectral_back(
                keeps, gots, at, legendre, some[0], remap_mat, devices, before, skip, ()
            )
            before, skip = [back], len(some)
        return back, mark

    def inverse(group, arrived, total, dtype, *after):
        at = Rows(lats, levels, len(group))
        rows = []
        for c, chunk in enumerate(members):
            shared = [u - chunk[0] for u in group if u in chunk]
            if shared:
                rows.append(waves[c][shared[0] * LANES : (shared[-1] + 1) * LANES])
        coef = arrived.reshape(LANES, at.lanes)
        return inverse_dft(coef, at, jnp.concatenate(rows), total, lats, dtype, after)

    def all_new():
        updated = jnp.concatenate([new[u] for u in range(units)]).reshape(owned, 2, lead, degrees)
        return updated[:, :, :levels].reshape(owned, 2 * levels, degrees)

    if len(sizes) == 3:
        coef_a, _ = dft(0)
        got_a = exchange(coef_a)
        coef_b, _ = dft(1)
        got_b = exchange(gate(coef_b, got_a))
        coef_c, _ = dft(2, got_a)
        adjoint(0, got_a)
        gradient_step(members[0])
        got_c = exchange(gate(coef_c, got_b, back_other[0]))
        adjoint(1, got_b)
        gradient_step(members[1][:-1])
        early, middle, late = members[0] + members[1][:1], members[1][1:] + members[2][:1], members[2][1:]
        back_a, mark = forward(early)
        gradient_step(members[1][-1:], mark)
        arrived_a = exchange(gate(back_a, got_c, back_other[members[1][-2]], other[members[1][-1]]))
        adjoint(2, got_c)
        gradient_step(members[2])
        back_b, _ = forward(middle, 2)
        arrived_b = exchange(gate(back_b, arrived_a, own[members[2][-1]]))
        back_c, _ = forward(late)
        total = inverse(early, arrived_a, None, jnp.float32)
        arrived_c = exchange(gate(back_c, arrived_b, total))
        updated = all_new()
        total = inverse(middle, arrived_b, total, jnp.float32)
        total = inverse(late, arrived_c, total, jnp.bfloat16)
    else:
        coef, _ = dft(0)
        adjoint(0, exchange(coef))
        gradient_step(members[0])
        updated = all_new()
        back, _ = forward(members[0])
        total = inverse(members[0], exchange(back), None, jnp.bfloat16)
    increment = jnp.transpose(total, (1, 0, 2))
    return (updated[None], increment[None])


def make_waves(owner_slots, lon_count):
    longitude = lax.iota(jnp.int32, lon_count)
    phases = longitude[:, None] * owner_slots[None, :] % lon_count
    angles = phases.astype(jnp.float32) * (2.0 * math.pi / lon_count)
    factor = math.sqrt(2.0 / lon_count)
    return jnp.stack([jnp.cos(angles), jnp.sin(angles)], axis=1) * factor


def plain_local(grad_grid, remap, modes, balance, legendre, control, step_size, owner_slots):
    lat_rows = grad_grid.shape[1]
    levels = grad_grid.shape[2]
    lon_count = grad_grid.shape[3]
    wave_count = owner_slots.shape[0]
    owned_count = legendre.shape[0]
    degrees = legendre.shape[2]
    wave_table = make_waves(owner_slots, lon_count)
    remap_var = remap[0]
    modes_var = modes[0]
    lifted = jnp.einsum(
        "ik,lij->lkj", remap_var, grad_grid[0].astype(jnp.float32), precision=highest
    )
    slab_coef = jnp.einsum("lkj,jcs->slck", lifted, wave_table, precision=highest)
    spectral_coef = jnp.einsum(
        "sln,slq->sqn",
        legendre,
        lax.all_to_all(
            slab_coef.reshape(wave_count, lat_rows, 2 * levels),
            "lat",
            split_axis=0,
            concat_axis=1,
            tiled=True,
        ),
        precision=highest,
    )
    spec_four = spectral_coef.reshape(owned_count, 2, levels, degrees)
    partner = from_behind(spec_four, "var", -1)
    blended = spec_four + jnp.einsum("ik,scin->sckn", balance, partner, precision=highest)
    spectral_coef = jnp.einsum("ik,scin->sckn", modes_var, blended, precision=highest).reshape(
        owned_count, 2 * levels, degrees
    )
    own_control = control[0]
    updated = own_control - step_size[0] * (own_control + spectral_coef)
    level_coef = jnp.einsum(
        "ki,scin->sckn",
        modes_var,
        updated.reshape(owned_count, 2, levels, degrees),
        precision=highest,
    )
    partner = from_behind(level_coef, "var", 1)
    level_coef = level_coef + jnp.einsum("ki,scin->sckn", balance, partner, precision=highest)
    level_coef = level_coef.reshape(owned_count, 2 * levels, degrees)
    fourier = jnp.einsum("sln,sqn->slq", legendre, level_coef, precision=highest)
    slab_back = lax.all_to_all(fourier, "lat", split_axis=1, concat_axis=0, tiled=True)
    slab_back = slab_back.reshape(wave_count, lat_rows, 2, levels)
    lowered = jnp.einsum("slck,jcs->lkj", slab_back, wave_table, precision=highest)
    increment = jnp.einsum("ik,lkj->lij", remap_var, lowered, precision=highest).astype(
        jnp.bfloat16
    )
    return (updated[None], increment[None])


def local(*arrays):
    grad_grid, legendre = arrays[0], arrays[4]
    devices = legendre.shape[1] // grad_grid.shape[1]
    levels = grad_grid.shape[2]
    tail = grad_grid.shape[1] * levels % LANES
    fits = (
        legendre.shape[0] % 4 == 0
        and grad_grid.shape[1] % 16 == 0
        and devices * 8 == LANES
        and round_up(levels, 8) <= LANES
        and tail > 0
        and grad_grid.shape[3] % 4 == 0
        and LANES % tail == 0
    )
    return (tiled_local if fits else plain_local)(*arrays)


def solution(mesh):
    return jax.shard_map(
        local,
        mesh=mesh,
        in_specs=(
            P("var", "lat", None, None),
            P("var", None, None),
            P("var", None, None),
            P(),
            P("lat", None, None),
            P("var", "lat", None, None),
            P("var"),
            P(),
        ),
        out_specs=(P("var", "lat", None, None), P("var", "lat", None, None)),
        check_vma=False,
    )
```

```python
import copy
import functools
import math

import jax
import jax.numpy as jnp
from jax import lax
from jax.experimental import pallas as pl
from jax.experimental.pallas import tpu as pltpu
from jax.sharding import PartitionSpec as P

highest = lax.Precision.HIGHEST
LANES = 128
COST_SHARE = 8
VMEM_BYTES = 63 * 1024 * 1024
NN = (((1,), (0,)), ((), ()))
NT = (((1,), (1,)), ((), ()))


def round_up(value, step):
    return -(-value // step) * step


def from_behind(block, axis, distance):
    devices = range(lax.axis_size(axis))
    route = [(i - distance, i) for i in devices if i - distance in devices]
    return lax.ppermute(block, axis, route)


def sine(x):
    square = x * x
    tail = 1.0
    for divisor in (156, 110, 72, 42, 20, 6):
        tail = 1.0 - square * (tail * (1.0 / divisor))
    return x * tail


def wave_rows(slots, lons):
    shape = (slots.shape[0], lons)
    lon = lax.broadcasted_iota(jnp.int32, shape, 1)
    part = lax.broadcasted_iota(jnp.int32, shape, 0) % 2
    phase = (slots * lon - part * (lons // 4)).astype(jnp.float32)
    phase = phase - jnp.floor(phase * (1.0 / lons)) * lons
    half = sine((phase - lons / 2) * (math.pi / lons))
    return (2.0 * half * half - 1.0) * math.sqrt(2.0 / lons)


def halves(x):
    upper = x.astype(jnp.bfloat16)
    return upper, (x - upper.astype(jnp.float32)).astype(jnp.bfloat16)


def mxu(a, b, dims):
    return lax.dot_general(a, b, dims, preferred_element_type=jnp.float32)


def dot3(a, b, dims=NN):
    (a_up, a_low), (b_up, b_low) = a, b
    return mxu(a_up, b_up, dims) + (mxu(a_up, b_low, dims) + mxu(a_low, b_up, dims))


def anywhere(arrays):
    return [pl.BlockSpec(memory_space=pl.ANY)] * len(arrays)


def behind(kernel, inputs, after):
    def body(*refs):
        kernel(*refs[:inputs], *refs[inputs + after :])

    return body


MARK = jax.ShapeDtypeStruct((8, LANES), jnp.float32)
MARK_SPEC = pl.BlockSpec(MARK.shape, lambda *_: (0, 0))


def cost(flops):
    return pl.CostEstimate(flops=flops // COST_SHARE, bytes_accessed=0, transcendentals=0)


def gate(block, *after):
    return pl.pallas_call(
        lambda *refs: None,
        in_specs=anywhere((block, *after)),
        out_specs=pl.BlockSpec(memory_space=pl.ANY),
        out_shape=jax.ShapeDtypeStruct(block.shape, block.dtype),
        input_output_aliases={0: 0},
        cost_estimate=pl.CostEstimate(flops=0, bytes_accessed=0, transcendentals=0),
        name="gate",
    )(block, *after)


class Rows:
    def __init__(self, lats, levels, units):
        self.levels, self.units = levels, units
        self.full = lats * levels // LANES * LANES
        self.tail = lats * levels - self.full
        self.lanes = units * self.full + round_up(units * self.tail, LANES)

    def end(self, unit):
        return self.units * self.full + unit * self.tail

    def pieces(self, unit, lat):
        first, last = lat * self.levels, (lat + 1) * self.levels
        pieces = []
        if first < self.full:
            stop = min(last, self.full)
            pieces.append((slice(unit * self.full + first, unit * self.full + stop), slice(0, stop - first)))
        if last > self.full:
            start = max(first, self.full)
            lane = self.end(unit) + start - self.full
            pieces.append((slice(lane, lane + last - start), slice(start - first, self.levels)))
        return pieces


def dft_kernel(steps, place, slot_ref, grad_ref, out_ref, wave_ref, mark_ref, rows_ref, right_ref):
    mark_ref[...] = jnp.zeros(mark_ref.shape, jnp.float32)
    levels, lats, lons = grad_ref.shape
    waves = wave_ref.shape[0]
    lead = rows_ref.shape[1] // lats

    @pl.when(pl.program_id(0) == 0)
    def _():
        for unit in range(place.units):
            at = slice(unit * LANES, (unit + 1) * LANES)
            rows = wave_rows(slot_ref[at, :], lons)
            wave_ref[at, :lons], wave_ref[at, lons:] = halves(rows)
            high, rest = halves(rows.T)
            right_ref[:, at] = high
            right_ref[:, waves + unit * LANES : waves + (unit + 1) * LANES] = rest

    grad = grad_ref[...].reshape(levels * lats, lons)
    terms = mxu(grad, right_ref[...], NN)
    coef = terms[:, :waves] + terms[:, waves:]
    for unit in range(place.units):
        rows_ref[unit, 0 : levels * lats, :] = coef[:, unit * LANES : (unit + 1) * LANES]
        if lead > levels:
            rows_ref[unit, levels * lats :, :] = jnp.zeros(((lead - levels) * lats, LANES), jnp.float32)

    for step in range(steps):

        @pl.when(pl.program_id(0) == step)
        def _(step=step):
            if step == 0:
                end = place.end(place.units)
                out_ref[:, end:] = jnp.zeros((LANES, place.lanes - end), jnp.float32)
            for unit in range(place.units):
                for lat in range(lats):
                    part = rows_ref[unit, pl.ds(lat, lead, stride=lats), :].T
                    for lanes, chosen in place.pieces(unit, step * lats + lat):
                        out_ref[:, lanes] = part[:, chosen]


def forward_dft(slots, grad, place, after):
    levels, lats, lons = grad.shape
    waves = slots.shape[0]
    block = 16
    steps = lats // block
    lead = round_up(levels, 8)
    return pl.pallas_call(
        behind(functools.partial(dft_kernel, steps, place), 2, len(after)),
        grid=(steps,),
        in_specs=[
            pl.BlockSpec(slots.shape, lambda i: (0, 0)),
            pl.BlockSpec((levels, block, lons), lambda i: (0, i, 0)),
            *anywhere(after),
        ],
        out_specs=[
            pl.BlockSpec((LANES, place.lanes), lambda i: (0, 0)),
            pl.BlockSpec((waves, 2 * lons), lambda i: (0, 0)),
            MARK_SPEC,
        ],
        out_shape=[
            jax.ShapeDtypeStruct((LANES, place.lanes), jnp.float32),
            jax.ShapeDtypeStruct((waves, 2 * lons), jnp.bfloat16),
            MARK,
        ],
        scratch_shapes=[
            pltpu.VMEM((place.units, lead * block, LANES), jnp.float32),
            pltpu.VMEM((lons, 2 * waves), jnp.bfloat16),
        ],
        compiler_params=pltpu.CompilerParams(vmem_limit_bytes=VMEM_BYTES),
        cost_estimate=cost(4 * levels * lats * lons * waves),
        name="forward_dft",
    )(slots, grad, *after)


def spectral_kernel(place, got_ref, end_ref, leg_ref, mat_ref, own_ref, send_ref, flat_ref, cols_ref):
    devices, rows, width = got_ref.shape
    slots, lat_count, _ = leg_ref.shape
    lats = lat_count // devices
    lead = mat_ref.shape[1] // 2
    levels = place.levels
    tiles = width // LANES
    cols_ref[...] = jnp.zeros(cols_ref.shape, jnp.float32)
    for tile in range(tiles):
        piece = got_ref[:, :, tile * LANES : (tile + 1) * LANES]
        flat_ref[tile] = piece.reshape(devices * rows, LANES)
    flat_ref[tiles] = end_ref[...].reshape(devices * rows, LANES)
    mat = halves(mat_ref[...])
    for slot in range(slots):
        turned = []
        for part in range(2):
            row = 2 * slot + part
            lines = [flat_ref[t, pl.ds(row, devices, stride=rows), :] for t in range(tiles + 1)]
            end = place.end(place.unit) % LANES
            lines[tiles] = lines[tiles][:, end : end + place.tail]
            line = jnp.concatenate(lines, axis=1)
            for lat in range(lats):
                cols_ref[pl.ds(row * lat_count + lat, devices, stride=lats), 0:levels] = line[
                    :, lat * levels : (lat + 1) * levels
                ]
            turned.append(cols_ref[row * lat_count : (row + 1) * lat_count, :].T[:lead])
        coef = dot3(halves(jnp.concatenate(turned, axis=0)), halves(leg_ref[slot]))
        mixed = dot3(mat, halves(coef))
        own_ref[slot] = mixed[: 2 * lead]
        send_ref[slot] = mixed[2 * lead :]


def spectral(got, place, unit, legendre, first, mat, after):
    devices, rows, _ = got.shape
    _, lat_count, degrees = legendre.shape
    slots = rows // 2
    lead = mat.shape[1]
    place = copy.copy(place)
    place.unit = unit
    end_tile = place.end(unit) // LANES
    shape = jax.ShapeDtypeStruct((slots, lead, degrees), jnp.float32)
    spec = pl.BlockSpec(shape.shape, lambda i: (0, 0, 0))
    return pl.pallas_call(
        behind(functools.partial(spectral_kernel, place), 4, len(after)),
        grid=(1,),
        in_specs=[
            pl.BlockSpec((devices, rows, place.full), lambda i: (0, 0, unit)),
            pl.BlockSpec((devices, rows, LANES), lambda i: (0, 0, end_tile)),
            pl.BlockSpec((slots, lat_count, degrees), lambda i: (first, 0, 0)),
            pl.BlockSpec(mat.shape, lambda i: (0, 0)),
            *anywhere(after),
        ],
        out_specs=[spec, spec],
        out_shape=[shape, shape],
        scratch_shapes=[
            pltpu.VMEM((place.full // LANES + 1, devices * rows, LANES), jnp.float32),
            pltpu.VMEM((rows * lat_count, LANES), jnp.float32),
        ],
        compiler_params=pltpu.CompilerParams(vmem_limit_bytes=VMEM_BYTES),
        cost_estimate=cost(12 * slots * lat_count * degrees * lead),
        name="spectral_adjoint",
    )(got, got, legendre, mat, *after)


def update_kernel(step_ref, own_ref, got_ref, control_ref, mode_ref, mat_ref, new_ref, keep_ref, send_ref):
    lead = own_ref.shape[1]
    mode = halves(mode_ref[...])
    mat = halves(mat_ref[...])
    for slot in range(own_ref.shape[0]):
        adjoint = dot3(mode, halves(own_ref[slot] + got_ref[slot]))
        control = control_ref[slot]
        new = control - step_ref[0] * (control + adjoint)
        new_ref[slot] = new
        mixed = dot3(mat, halves(new))
        keep_ref[slot] = mixed[:lead]
        send_ref[slot] = mixed[lead:]


def update(step_size, own, got, control, first, mode, mat, after):
    slots, lead, degrees = own.shape
    spec = pl.BlockSpec(own.shape, lambda i: (0, 0, 0))
    shape = jax.ShapeDtypeStruct(own.shape, jnp.float32)
    return pl.pallas_call(
        behind(update_kernel, 6, len(after)),
        grid=(1,),
        in_specs=[
            pl.BlockSpec(memory_space=pltpu.SMEM),
            spec,
            spec,
            pl.BlockSpec(own.shape, lambda i: (first, 0, 0)),
            pl.BlockSpec(mode.shape, lambda i: (0, 0)),
            pl.BlockSpec(mat.shape, lambda i: (0, 0)),
            *anywhere(after),
        ],
        out_specs=[spec, spec, spec],
        out_shape=[shape, shape, shape],
        compiler_params=pltpu.CompilerParams(vmem_limit_bytes=VMEM_BYTES),
        cost_estimate=cost(36 * slots * lead * lead * degrees),
        name="gradient_step",
    )(step_size, own, got, control, mode, mat, *after)


def back_kernel(place, units, skip, *refs):
    keep_refs, got_refs = refs[:units], refs[units : 2 * units]
    leg_ref, mat_ref = refs[2 * units : 2 * units + 2]
    out_ref, mark_ref, cols_ref, line_ref, flat_ref = refs[-5:]
    mark_ref[...] = jnp.zeros(mark_ref.shape, jnp.float32)
    devices, rows, _ = out_ref.shape
    slots, lat_count, degrees = leg_ref.shape
    lats = lat_count // devices
    lead = mat_ref.shape[0] // 2
    levels = place.levels
    tiles = place.full // LANES
    mat = halves(mat_ref[...])
    gap = jnp.zeros((LANES - lead, degrees), jnp.float32)

    for unit in range(units):

        @pl.when(pl.program_id(0) == unit)
        def _(unit=unit):
            if unit == 0 and skip:
                out_ref[...] = refs[2 * units + 2][...]
            elif unit == 0:
                ends = place.units * place.full
                out_ref[:, :, ends:] = jnp.zeros((devices, rows, place.lanes - ends), jnp.float32)
            if place.tail:
                unused = (line_ref.shape[0], LANES - place.tail)
                line_ref[:, place.full + place.tail :] = jnp.zeros(unused, jnp.float32)
            for slot in range(slots):
                coef = dot3(mat, halves(keep_refs[unit][slot] + got_refs[unit][slot]))
                coef = jnp.concatenate([coef[:lead], gap, coef[lead:], gap], axis=0)
                fourier = dot3(halves(leg_ref[slot]), halves(coef), NT)
                for part in range(2):
                    row = 2 * slot + part
                    base = row * lat_count
                    cols_ref[base : base + lat_count, :] = fourier[:, part * LANES : (part + 1) * LANES]
                    line = slice(row * devices, (row + 1) * devices)
                    for lat in range(lats):
                        piece = cols_ref[pl.ds(base + lat, devices, stride=lats), :]
                        line_ref[line, lat * levels : (lat + 1) * levels] = piece[:, :levels]
                    for tile in range(line_ref.shape[1] // LANES):
                        flat_ref[tile, pl.ds(row, devices, stride=rows), :] = line_ref[
                            line, tile * LANES : (tile + 1) * LANES
                        ]
            for tile in range(tiles):
                start = (skip + unit) * place.full + tile * LANES
                out_ref[:, :, start : start + LANES] = flat_ref[tile].reshape(devices, rows, LANES)
            if place.tail:
                lane = place.end(skip + unit)
                ends = flat_ref[tiles].reshape(devices, rows, LANES)[:, :, : place.tail]
                out_ref[:, :, lane : lane + place.tail] = ends


def spectral_back(keeps, gots, place, legendre, first, mat, devices, before, skip, after):
    slots, lead, degrees = keeps[0].shape
    lat_count = legendre.shape[1]
    rows = 2 * slots
    units = len(keeps)
    spec = pl.BlockSpec(keeps[0].shape, lambda i: (0, 0, 0))
    padded_row = place.full + (LANES if place.tail else 0)
    shape = jax.ShapeDtypeStruct((devices, rows, place.lanes), jnp.float32)
    return pl.pallas_call(
        behind(
            functools.partial(back_kernel, place, units, skip), 2 * units + 2 + len(before), len(after)
        ),
        grid=(units,),
        in_specs=[spec] * (2 * units)
        + [
            pl.BlockSpec((slots, lat_count, degrees), lambda i: (i + first, 0, 0)),
            pl.BlockSpec(mat.shape, lambda i: (0, 0)),
            *[pl.BlockSpec(b.shape, lambda i: (0, 0, 0)) for b in before],
            *anywhere(after),
        ],
        out_specs=[pl.BlockSpec(shape.shape, lambda i: (0, 0, 0)), MARK_SPEC],
        out_shape=[shape, MARK],
        scratch_shapes=[
            pltpu.VMEM((rows * lat_count, LANES), jnp.float32),
            pltpu.VMEM((rows * devices, padded_row), jnp.float32),
            pltpu.VMEM((padded_row // LANES, devices * rows, LANES), jnp.float32),
        ],
        compiler_params=pltpu.CompilerParams(vmem_limit_bytes=VMEM_BYTES),
        cost_estimate=cost(12 * units * slots * lat_count * degrees * lead),
        name="spectral_forward",
    )(*keeps, *gots, legendre, mat, *before, *after)


def inverse_kernel(steps, place, has_total, coef_ref, up_ref, low_ref, *refs):
    total_ref = refs[0] if has_total else None
    out_ref, rows_ref, left_ref = refs[has_total:]
    levels, lats, columns = out_ref.shape
    waves = up_ref.shape[0]

    for step in range(steps):

        @pl.when(pl.program_id(0) == step)
        def _(step=step):
            for unit in range(place.units):
                for lat in range(lats):
                    parts = [coef_ref[:, at] for at, _ in place.pieces(unit, step * lats + lat)]
                    part = parts[0] if len(parts) == 1 else jnp.concatenate(parts, axis=1)
                    rows_ref[unit, pl.ds(lat, levels, stride=lats), :] = part.T
                high, rest = halves(rows_ref[unit])
                for term, value in enumerate((high, rest, high)):
                    start = term * waves + unit * LANES
                    left_ref[:, start : start + LANES] = value

    width = 512 if columns % 512 == 0 else columns
    for first in range(0, columns, width):
        at = slice(first, first + width)
        right = jnp.concatenate([up_ref[:, at], up_ref[:, at], low_ref[:, at]], axis=0)
        result = mxu(left_ref[...], right, NN).reshape(levels, lats, width)
        if has_total:
            result = result + total_ref[:, :, at]
        out_ref[:, :, at] = result.astype(out_ref.dtype)


def inverse_dft(coef, place, table, total, lats, dtype, after):
    waves = table.shape[0]
    lons = table.shape[1] // 2
    levels = place.levels
    block = 16
    steps = lats // block
    grid_spec = pl.BlockSpec((levels, block, lons), lambda i: (0, i, 0))
    totals = [] if total is None else [total]
    return pl.pallas_call(
        behind(functools.partial(inverse_kernel, steps, place, len(totals)), 3 + len(totals), len(after)),
        grid=(steps,),
        in_specs=[
            pl.BlockSpec(coef.shape, lambda i: (0, 0)),
            pl.BlockSpec((waves, lons), lambda i: (0, 0)),
            pl.BlockSpec((waves, lons), lambda i: (0, 1)),
        ]
        + [grid_spec] * len(totals)
        + anywhere(after),
        out_specs=grid_spec,
        out_shape=jax.ShapeDtypeStruct((levels, lats, lons), dtype),
        scratch_shapes=[
            pltpu.VMEM((place.units, levels * block, LANES), jnp.float32),
            pltpu.VMEM((levels * block, 3 * waves), jnp.bfloat16),
        ],
        compiler_params=pltpu.CompilerParams(vmem_limit_bytes=VMEM_BYTES),
        cost_estimate=cost(6 * levels * lats * lons * waves),
        name="inverse_dft",
    )(coef, table, table, *totals, *after)


def padded(matrix, lead):
    return jnp.pad(matrix, ((0, lead - matrix.shape[0]), (0, lead - matrix.shape[1])))


def on_both(matrix, lead):
    return jnp.kron(jnp.eye(2, dtype=jnp.float32), padded(matrix, lead))


def exchange(block):
    return lax.all_to_all(block, "lat", split_axis=0, concat_axis=0, tiled=True)


def tiled_local(grad_grid, remap, modes, balance, legendre, control, step_size, owner_slots):
    _, lats, levels, lons = grad_grid.shape
    owned, _, degrees = legendre.shape
    wave_count = owner_slots.shape[0]
    devices = wave_count // owned
    lead = round_up(levels, 8)
    grad = jnp.transpose(grad_grid[0], (1, 0, 2))
    units = owned // 4
    sizes = [1, units - 3, 2] if units > 3 else [units]
    place = [Rows(lats, levels, size) for size in sizes]
    members, first = [], 0
    for size in sizes:
        members.append(list(range(first, first + size)))
        first += size
    by_owner = owner_slots.reshape(devices, units, 4).transpose(1, 0, 2)

    row_slots = jnp.repeat(by_owner.reshape(units * LANES // 2), 2)[:, None]
    waves = {}
    mix = functools.partial(jnp.einsum, precision=highest)
    adjoint_mat = jnp.concatenate(
        [on_both(remap[0].T, lead), on_both(mix("ik,kj->ji", remap[0], balance), lead)]
    )
    mode_mat = on_both(modes[0].T, lead)
    forward_mat = jnp.concatenate(
        [on_both(modes[0], lead), on_both(mix("ik,kj->ij", balance, modes[0]), lead)]
    )
    remap_mat = on_both(remap[0], lead)
    own_control = control[0].reshape(owned, 2, levels, degrees)
    own_control = jnp.pad(own_control, ((0, 0), (0, 0), (0, lead - levels), (0, 0)))
    own_control = own_control.reshape(owned, 2 * lead, degrees)
    own, send, other, new, keep, back_send, back_other = ({} for _ in range(7))

    def dft(c, *after):
        rows = slice(members[c][0] * LANES, (members[c][-1] + 1) * LANES)
        coef, waves[c], mark = forward_dft(row_slots[rows], grad, place[c], after)
        return coef.reshape(devices, 8, place[c].lanes), mark

    def adjoint(c, got, *after):
        for at, u in enumerate(members[c]):
            own[u], send[u] = spectral(got, place[c], at, legendre, u, adjoint_mat, after)
            other[u] = from_behind(send[u], "var", -1)
            after = (own[u],)

    def gradient_step(group, *after):
        for u in group:
            new[u], keep[u], back_send[u] = update(
                step_size, own[u], other[u], own_control, u, mode_mat, forward_mat, after
            )
            after = (new[u],)
            back_other[u] = from_behind(back_send[u], "var", 1)

    def forward(group, parts=1):
        at = Rows(lats, levels, len(group))
        before, skip = [], 0
        for some in [group] if parts == 1 else [group[:-1], group[-1:]]:
            keeps, gots = [keep[u] for u in some], [back_other[u] for u in some]
            back, mark = spectral_back(
                keeps, gots, at, legendre, some[0], remap_mat, devices, before, skip, ()
            )
            before, skip = [back], len(some)
        return back, mark

    def inverse(group, arrived, total, dtype, *after):
        at = Rows(lats, levels, len(group))
        rows = []
        for c, chunk in enumerate(members):
            shared = [u - chunk[0] for u in group if u in chunk]
            if shared:
                rows.append(waves[c][shared[0] * LANES : (shared[-1] + 1) * LANES])
        coef = arrived.reshape(LANES, at.lanes)
        return inverse_dft(coef, at, jnp.concatenate(rows), total, lats, dtype, after)

    def all_new():
        updated = jnp.concatenate([new[u] for u in range(units)]).reshape(owned, 2, lead, degrees)
        return updated[:, :, :levels].reshape(owned, 2 * levels, degrees)

    if len(sizes) == 3:
        coef_a, _ = dft(0)
        got_a = exchange(coef_a)
        coef_b, _ = dft(1)
        got_b = exchange(gate(coef_b, got_a))
        coef_c, _ = dft(2, got_a)
        adjoint(0, got_a)
        gradient_step(members[0])
        got_c = exchange(gate(coef_c, got_b, back_other[0]))
        adjoint(1, got_b)
        gradient_step(members[1][:-1])
        early, middle, late = members[0] + members[1][:1], members[1][1:] + members[2][:1], members[2][1:]
        back_a, mark = forward(early)
        gradient_step(members[1][-1:], mark)
        arrived_a = exchange(gate(back_a, got_c, other[members[1][-1]]))
        adjoint(2, got_c)
        gradient_step(members[2])
        back_b, _ = forward(middle, 2)
        arrived_b = exchange(gate(back_b, arrived_a, own[members[2][-1]]))
        back_c, _ = forward(late)
        total = inverse(early, arrived_a, None, jnp.float32)
        arrived_c = exchange(gate(back_c, arrived_b, total))
        updated = all_new()
        total = inverse(middle, arrived_b, total, jnp.float32)
        total = inverse(late, arrived_c, total, jnp.bfloat16)
    else:
        coef, _ = dft(0)
        adjoint(0, exchange(coef))
        gradient_step(members[0])
        updated = all_new()
        back, _ = forward(members[0])
        total = inverse(members[0], exchange(back), None, jnp.bfloat16)
    increment = jnp.transpose(total, (1, 0, 2))
    return (updated[None], increment[None])


def make_waves(owner_slots, lon_count):
    longitude = lax.iota(jnp.int32, lon_count)
    phases = longitude[:, None] * owner_slots[None, :] % lon_count
    angles = phases.astype(jnp.float32) * (2.0 * math.pi / lon_count)
    factor = math.sqrt(2.0 / lon_count)
    return jnp.stack([jnp.cos(angles), jnp.sin(angles)], axis=1) * factor


def plain_local(grad_grid, remap, modes, balance, legendre, control, step_size, owner_slots):
    lat_rows = grad_grid.shape[1]
    levels = grad_grid.shape[2]
    lon_count = grad_grid.shape[3]
    wave_count = owner_slots.shape[0]
    owned_count = legendre.shape[0]
    degrees = legendre.shape[2]
    wave_table = make_waves(owner_slots, lon_count)
    remap_var = remap[0]
    modes_var = modes[0]
    lifted = jnp.einsum(
        "ik,lij->lkj", remap_var, grad_grid[0].astype(jnp.float32), precision=highest
    )
    slab_coef = jnp.einsum("lkj,jcs->slck", lifted, wave_table, precision=highest)
    spectral_coef = jnp.einsum(
        "sln,slq->sqn",
        legendre,
        lax.all_to_all(
            slab_coef.reshape(wave_count, lat_rows, 2 * levels),
            "lat",
            split_axis=0,
            concat_axis=1,
            tiled=True,
        ),
        precision=highest,
    )
    spec_four = spectral_coef.reshape(owned_count, 2, levels, degrees)
    partner = from_behind(spec_four, "var", -1)
    blended = spec_four + jnp.einsum("ik,scin->sckn", balance, partner, precision=highest)
    spectral_coef = jnp.einsum("ik,scin->sckn", modes_var, blended, precision=highest).reshape(
        owned_count, 2 * levels, degrees
    )
    own_control = control[0]
    updated = own_control - step_size[0] * (own_control + spectral_coef)
    level_coef = jnp.einsum(
        "ki,scin->sckn",
        modes_var,
        updated.reshape(owned_count, 2, levels, degrees),
        precision=highest,
    )
    partner = from_behind(level_coef, "var", 1)
    level_coef = level_coef + jnp.einsum("ki,scin->sckn", balance, partner, precision=highest)
    level_coef = level_coef.reshape(owned_count, 2 * levels, degrees)
    fourier = jnp.einsum("sln,sqn->slq", legendre, level_coef, precision=highest)
    slab_back = lax.all_to_all(fourier, "lat", split_axis=1, concat_axis=0, tiled=True)
    slab_back = slab_back.reshape(wave_count, lat_rows, 2, levels)
    lowered = jnp.einsum("slck,jcs->lkj", slab_back, wave_table, precision=highest)
    increment = jnp.einsum("ik,lkj->lij", remap_var, lowered, precision=highest).astype(
        jnp.bfloat16
    )
    return (updated[None], increment[None])


def local(*arrays):
    grad_grid, legendre = arrays[0], arrays[4]
    devices = legendre.shape[1] // grad_grid.shape[1]
    levels = grad_grid.shape[2]
    tail = grad_grid.shape[1] * levels % LANES
    fits = (
        legendre.shape[0] % 4 == 0
        and grad_grid.shape[1] % 16 == 0
        and devices * 8 == LANES
        and round_up(levels, 8) <= LANES
        and tail > 0
        and grad_grid.shape[3] % 4 == 0
        and LANES % tail == 0
    )
    return (tiled_local if fits else plain_local)(*arrays)


def solution(mesh):
    return jax.shard_map(
        local,
        mesh=mesh,
        in_specs=(
            P("var", "lat", None, None),
            P("var", None, None),
            P("var", None, None),
            P(),
            P("lat", None, None),
            P("var", "lat", None, None),
            P("var"),
            P(),
        ),
        out_specs=(P("var", "lat", None, None), P("var", "lat", None, None)),
        check_vma=False,
    )
```
